256 devices in a mesh: kv: 32 (over z, x), head: 8 (over y, core).
Axes of the slice: x: 4, y: 4, z: 8, core: 2. Of those that a mesh axis runs over, the one named last changes fastest.
Arguments:
- tokens: bfloat16 [2, 8, 8192], P(None, None, 'kv'), may hold values from -3 to 3
- norm_attn: bfloat16 [8192], P('kv'), may hold values from 0.099609375 to 1.8984375
- norm_ffn: bfloat16 [8192], P('kv'), may hold values from 0.099609375 to 1.8984375
- w_query: bfloat16 [8192, 8192], P('kv', 'head'), may hold values from -0.0625 to 0.0625
- w_kv: bfloat16 [8192, 2, 1024], P('kv', None, 'head'), may hold values from -0.0625 to 0.0625
- w_out: bfloat16 [8192, 8192], P('head', 'kv'), may hold values from -0.0625 to 0.0625
- w_gate_up: bfloat16 [8192, 2, 28672], P('kv', None, 'head'), may hold values from -0.0625 to 0.0625
- w_down: bfloat16 [28672, 8192], P('head', 'kv'), may hold values from -0.03125 to 0.03125
- cache_keys: bfloat16 [8, 8, 32768, 128], P(None, 'head', 'kv'), may hold values from -400 to 400
- cache_values: bfloat16 [8, 8, 32768, 128], P(None, 'head', 'kv'), may hold values from -6 to 6
- lengths: int32 [8], replicated, may hold values from 4096 to 32768, as said below
- owner: int32 [2], replicated, may hold values from 0 to 31
Outputs:
- layer_out: bfloat16 [2, 8, 8192], P(None, None, 'kv')
- stored: bfloat16 [32, 2, 8, 8, 2, 128], P('kv', None, None, 'head')
The draws below stay inside these ranges and needn't reach their ends.
Inputs may be any that keep to these rules, and one draw needn't show every extreme that they name: `lengths`: at least one rollout has all 32768 positions cached.
All inputs are finite; a program needn't handle non-finite values.
Results may differ from the reference program's by a relative error of at most 0.014.
The reference program's roundings to bfloat16 on the way count: a program that leaves them out, or rounds other values in their place, can miss the bound.
Values may be sent and summed in bfloat16 or wider, within the bound.
No kernel may reach another device: no remote copies, remote signals or barrier semaphores. Data moves between devices by JAX's collectives and lax.ppermute only.
A program may use at most 64 MiB of HBM per device.

```python
import jax
import jax.numpy as jnp
from jax import lax

D = 8192
QH = 64
KVH = 8
HD = 128
FF = 28672
STEPS = 2
B = 8
CTX = 32768
KV_DEVS = 32


def draw_cache_keys(key, part):
    key = jax.random.fold_in(key, 11)
    first = jax.random.fold_in(key, 0)
    base = 3.0 * jax.random.normal(first, (B, KVH, CTX, HD), jnp.float32)
    return jnp.clip(base, -400.0, 400.0).astype(jnp.bfloat16)


def draw_lengths(key, part):
    key = jax.random.fold_in(key, 5)
    first, second = jax.random.split(key)
    spread = jax.random.randint(first, (B,), CTX // 8, CTX + 1)
    picked = jax.random.randint(second, (), 0, B)
    return jnp.where(jnp.arange(B) == picked, CTX, spread).astype(jnp.int32)


def block_levels(stream_key, dims, pieces, low, high):
    factor_of = 1.0
    for axis_at, shards_of in pieces:
        draws = jax.random.uniform(jax.random.fold_in(jax.random.fold_in(stream_key, 6), axis_at), (shards_of,), jnp.float32, low / len(pieces), high / len(pieces))
        factor_of = factor_of * jnp.repeat(jnp.exp(draws), dims[axis_at] // shards_of).reshape((-1,) + (1,) * (len(dims) - 1 - axis_at))
    return factor_of


def bell_draw(key, dims, scale, reach, cuts=(), kind=jnp.bfloat16):
    entries = jax.random.normal(key, dims, jnp.float32) * scale
    if len(cuts) > 0:
        entries = block_levels(key, dims, cuts, -0.22, 0.18) * entries
    return jnp.clip(entries, min=-reach, max=reach).astype(kind)


def setup_inputs(seed: int = 0) -> dict:
    splits = jax.random.split(jax.random.key(seed), 13)
    tokens = bell_draw(splits[0], (STEPS, B, D), 0.5, 3.0, ((2, 32),))
    norm_attn = jnp.clip(1.0 + 0.18 * jax.random.normal(splits[1], (D,), jnp.float32), 0.099609375, 1.8984375).astype(jnp.bfloat16)
    norm_ffn = jnp.clip(1.0 + 0.18 * jax.random.normal(splits[2], (D,), jnp.float32), 0.099609375, 1.8984375).astype(jnp.bfloat16)
    w_query = bell_draw(splits[3], (D, QH * HD), D ** -0.5, 0.0625, ((0, 32), (1, 8)))
    w_kv = bell_draw(splits[4], (D, 2, KVH * HD), D ** -0.5, 0.0625, ((0, 32), (2, 8)))
    w_out = bell_draw(splits[5], (QH * HD, D), (QH * HD) ** -0.5, 0.0625, ((0, 8), (1, 32)))
    w_gate_up = bell_draw(splits[6], (D, 2, FF), D ** -0.5, 0.0625, ((0, 32), (2, 8)))
    w_down = bell_draw(splits[7], (FF, D), FF ** -0.5, 0.03125, ((0, 8), (1, 32)))
    cache_keys = draw_cache_keys(jax.random.fold_in(splits[12], 71), 0)
    cache_values = bell_draw(splits[9], (B, KVH, CTX, HD), 1.0, 6.0, ((1, 8), (2, 32)))
    lengths = draw_lengths(jax.random.fold_in(splits[12], 71), 0)
    owner = jax.random.randint(splits[11], (STEPS,), 0, KV_DEVS).astype(jnp.int32)
    return {"tokens": tokens, "norm_attn": norm_attn, "norm_ffn": norm_ffn, "w_query": w_query, "w_kv": w_kv, "w_out": w_out, "w_gate_up": w_gate_up, "w_down": w_down, "cache_keys": cache_keys, "cache_values": cache_values, "lengths": lengths, "owner": owner}


EPSILON = 1e-05
NEGATIVE = -1e+30

def reference(tokens, norm_attn, norm_ffn, w_query, w_kv, w_out, w_gate_up, w_down, cache_keys, cache_values, lengths, owner):
    row_count = STEPS * B
    group = QH // KVH
    flat = tokens.astype(jnp.float32).reshape(row_count, D)
    inv_attn = lax.rsqrt(lax.optimization_barrier(jnp.mean(flat * flat, -1)) + EPSILON)[:, None]
    normed = (flat * norm_attn.astype(jnp.float32)).astype(jnp.bfloat16)
    query = (jnp.dot(normed, w_query, preferred_element_type=jnp.float32) * inv_attn).astype(jnp.bfloat16)
    query = query.reshape(STEPS, B, KVH, group, HD)
    fresh = (jnp.dot(normed, w_kv.reshape(D, 2 * KVH * HD), preferred_element_type=jnp.float32) * inv_attn).astype(jnp.bfloat16)
    fresh = fresh.reshape(STEPS, B, 2, KVH, HD)
    scale = HD ** (-0.5)
    step_ids = jnp.arange(STEPS, dtype=jnp.int32)
    causal = step_ids[None, :] <= step_ids[:, None]
    positions = jnp.arange(CTX, dtype=jnp.int32)

    def per_rollout(items):
        q_roll, k_roll, v_roll, length, new_keys, new_values = items
        q_wide = q_roll.astype(jnp.float32)
        older = jnp.einsum('sngd,ncd->sngc', q_wide, k_roll.astype(jnp.float32)) * scale
        keep_old = (positions < length)[None, None, None, :]
        newer = jnp.einsum('sngd,tnd->sngt', q_wide, new_keys.astype(jnp.float32)) * scale
        keep_new = causal[:, None, None, :]
        older = jnp.where(keep_old, older, NEGATIVE)
        newer = jnp.where(keep_new, newer, NEGATIVE)
        top = jnp.maximum(lax.optimization_barrier(jnp.max(older, -1)), lax.optimization_barrier(jnp.max(newer, -1)))
        e_old = jnp.where(keep_old, jnp.exp(older - top[..., None]), 0.0)
        e_new = jnp.where(keep_new, jnp.exp(newer - top[..., None]), 0.0)
        total = lax.optimization_barrier(jnp.sum(e_old, -1)) + lax.optimization_barrier(jnp.sum(e_new, -1))
        weighted = jnp.einsum('sngc,ncd->sngd', e_old.astype(jnp.bfloat16).astype(jnp.float32), v_roll.astype(jnp.float32))
        weighted = weighted + jnp.einsum('sngt,tnd->sngd', e_new.astype(jnp.bfloat16).astype(jnp.float32), new_values.astype(jnp.float32))
        return (weighted / total[..., None]).astype(jnp.bfloat16)
    context = lax.map(per_rollout, (query.transpose(1, 0, 2, 3, 4), cache_keys, cache_values, lengths, fresh[:, :, 0].transpose(1, 0, 2, 3), fresh[:, :, 1].transpose(1, 0, 2, 3)))
    attended = context.transpose(1, 0, 2, 3, 4).reshape(row_count, QH * HD)
    resid = flat + jnp.dot(attended, w_out, preferred_element_type=jnp.float32)
    inv_ffn = lax.rsqrt(lax.optimization_barrier(jnp.mean(resid * resid, -1)) + EPSILON)[:, None, None]
    normed_two = (resid * norm_ffn.astype(jnp.float32)).astype(jnp.bfloat16)
    gate_up = jnp.dot(normed_two, w_gate_up.reshape(D, 2 * FF), preferred_element_type=jnp.float32).reshape(row_count, 2, FF) * inv_ffn
    hidden = (jax.nn.silu(gate_up[:, 0]) * gate_up[:, 1]).astype(jnp.bfloat16)
    layer_out = (resid + jnp.dot(hidden, w_down, preferred_element_type=jnp.float32)).astype(jnp.bfloat16).reshape(STEPS, B, D)
    chosen = jnp.arange(KV_DEVS, dtype=jnp.int32)[:, None] == owner[None, :]
    stored = jnp.where(chosen[:, :, None, None, None, None], fresh.transpose(0, 1, 3, 2, 4)[None], jnp.zeros((), jnp.bfloat16))
    return (layer_out, stored)
```

```python
import functools

import jax
import jax.numpy as jnp
from jax import lax
from jax.experimental import pallas as pl
from jax.experimental.pallas import tpu as pltpu
from jax.sharding import PartitionSpec as P

D = 8192
EPSILON = 1e-05
NEGATIVE = -1e30
F32 = jnp.float32
BF16 = jnp.bfloat16
LANES = 128
VMEM = pl.BlockSpec(memory_space=pltpu.VMEM)
SMEM = pl.BlockSpec(memory_space=pltpu.SMEM)
ANY = pl.BlockSpec(memory_space=pl.ANY)


def exchange(x, axis):
    return lax.all_to_all(x, axis, 0, 0, tiled=True)


def call(body, out_shape, args, specs=None, scratch=(), limit=24):
    return pl.pallas_call(
        body,
        out_shape=out_shape,
        in_specs=[VMEM] * len(args) if specs is None else specs,
        out_specs=jax.tree.map(lambda _: VMEM, out_shape),
        scratch_shapes=list(scratch),
        compiler_params=pltpu.CompilerParams(vmem_limit_bytes=int(limit * 2**20)),
    )(*args)


def project(
    tokens_at, gain_at, w_query_at, w_kv_at, out, tokens, gain, w_query, w_kv, wide, sems
):
    copies = [
        pltpu.make_async_copy(src, dst, sems.at[i])
        for i, (src, dst) in enumerate(
            ((w_kv_at, w_kv), (tokens_at, tokens), (gain_at, gain), (w_query_at, w_query))
        )
    ]
    for copy in copies:
        copy.start()
    for copy in copies[:3]:
        copy.wait()
    rows = tokens.shape[0] * tokens.shape[1]
    width = tokens.shape[2]
    wide[...] = w_kv[...].astype(F32).reshape(2 * width, LANES)
    flat = tokens[...].astype(F32).reshape(rows, tokens.shape[2])
    normed = (flat * gain[...].astype(F32).reshape(1, -1)).astype(BF16)
    kv = [
        jnp.dot(
            normed, wide[pl.ds(i, width, stride=2), :].astype(BF16), preferred_element_type=F32
        )
        for i in range(2)
    ]
    copies[3].wait()
    q = jnp.dot(normed, w_query[...], preferred_element_type=F32)
    stat = jnp.broadcast_to(jnp.sum(flat * flat, -1, keepdims=True), (rows, LANES))
    for half in range(2):
        for slot in range(8):
            if slot < 4:
                at = (half * 4 + slot) * LANES
                part = q[:, at : at + LANES]
            elif slot == 4:
                part = kv[half]
            else:
                part = stat
            out[pl.ds(half * 8 + slot, rows, stride=16), :] = part


def finish(got, relaid, out):
    total = jnp.sum(got[...], 0)
    inv = lax.rsqrt(total[7:8] / D + EPSILON)
    out[...] = jnp.broadcast_to((total * inv).astype(BF16)[None], out.shape)


def attend(lengths, owner, index, whole, keys, values, out, stored):
    rollouts, span, hd = keys.shape
    scale = hd ** (-0.5)
    row = lax.broadcasted_iota(jnp.int32, (8, LANES), 0)
    lane = lax.broadcasted_iota(jnp.int32, (16, LANES), 1)
    column = lax.broadcasted_iota(jnp.int32, (16, span), 1)
    step = lax.broadcasted_iota(jnp.int32, (16, 1), 0) // 8
    here = index[0] == 0
    queries, news = [], []
    for b in range(rollouts):
        tiles, pairs = [], []
        for s in range(2):
            low = whole[(s * rollouts + b) * 2].astype(F32)
            high = whole[(s * rollouts + b) * 2 + 1].astype(F32)
            tiles.append(jnp.where(row < 4, low, pltpu.roll(high, 4, 0)))
            pairs.append((low[4:5], high[4:5]))
            pair = jnp.concatenate(pairs[s], 0)
            mine = owner[s] == index[0]
            stored[0, s, b, 0] = jnp.where(mine, pair, jnp.zeros_like(pair)).astype(BF16)
        queries.append(jnp.concatenate(tiles, 0))
        news.append(pairs)
    scores = []
    for b in range(rollouts):
        scores.append(
            lax.dot_general(
                queries[b].astype(BF16),
                keys[b],
                (((1,), (1,)), ((), ())),
                preferred_element_type=F32,
            )
            * scale
        )
    weights, totals, tops, extras = [], [], [], []
    for b in range(rollouts):
        keep = column < lengths[b] - index[0] * span
        masked = jnp.where(keep, scores[b], NEGATIVE)
        top = jnp.max(masked, -1, keepdims=True)
        fresh = []
        for t in range(2):
            allowed = (step >= t) & here
            score = jnp.sum(queries[b] * news[b][t][0], -1, keepdims=True) * scale
            fresh.append((allowed, jnp.where(allowed, score, NEGATIVE)))
            top = jnp.maximum(top, fresh[t][1])
        e = jnp.where(keep, jnp.exp(masked - top), 0.0)
        extra = [jnp.where(ok, jnp.exp(score - top), 0.0) for ok, score in fresh]
        totals.append(jnp.sum(e, -1, keepdims=True) + extra[0] + extra[1])
        weights.append(e.astype(BF16))
        tops.append(top)
        extras.append(extra)
    for b in range(rollouts):
        sums = jnp.dot(weights[b], values[b], preferred_element_type=F32)
        for t in range(2):
            sums = sums + extras[b][t].astype(BF16).astype(F32) * news[b][t][1]
        stat = jnp.where(lane < LANES // 2, tops[b], totals[b])
        for s in range(2):
            sums_s, stat_s = sums[s * 8 : s * 8 + 8], stat[s * 8 : s * 8 + 8]
            at = (s * rollouts + b) * 2
            out[at] = jnp.where(row < 4, sums_s, pltpu.roll(stat_s, 4, 0))
            out[at + 1] = jnp.where(row < 4, pltpu.roll(sums_s, 4, 0), stat_s)


def combine(got, out):
    tops = got[:, 4:, :1]
    factor = jnp.exp(tops - jnp.max(tops, 0, keepdims=True))
    total = jnp.sum(factor * got[:, 4:, LANES // 2 : LANES // 2 + 1], 0)
    context = jnp.sum(factor * got[:, :4, :], 0) / total
    out[...] = jnp.broadcast_to(context.astype(BF16)[None], out.shape)


def gathered_dot(used, whole, w, out, wide):
    chunks, lines = whole.shape[:2]
    wide[...] = whole[...].astype(F32).reshape(chunks * lines, LANES)
    rows = chunks // 2
    parts = [
        wide[pl.ds(half * lines + slot, rows, stride=2 * lines), :].astype(BF16)
        for half in range(2)
        for slot in range(used)
    ]
    part = jnp.dot(jnp.concatenate(parts, 1), w[...], preferred_element_type=F32)
    out[...] = jnp.broadcast_to(part[None], out.shape)


def gate_up(got, tokens, gain, w, resid_out, out):
    rows, width = resid_out.shape
    resid = tokens[...].astype(F32).reshape(rows, width) + jnp.sum(got[...], 0)
    resid_out[...] = resid
    normed = (resid * gain[...].astype(F32).reshape(1, -1)).astype(BF16)
    stat = jnp.broadcast_to(jnp.sum(resid * resid, -1, keepdims=True), (rows, LANES))
    lines = w.shape[2] // 2 // LANES
    for which in range(2):
        part = jnp.dot(normed, w[which], preferred_element_type=F32)
        for half in range(2):
            for slot in range(16):
                at = (half * lines + slot) * LANES
                out[pl.ds(half * 32 + which * 16 + slot, rows, stride=64), :] = (
                    part[:, at : at + LANES] if slot < lines else stat
                )


def activate(got, out):
    total = jnp.sum(got[...], 0)
    inv = lax.rsqrt(total[15:16] / D + EPSILON)
    gate, up = total[:16] * inv, total[16:] * inv
    hidden = (gate * jax.nn.sigmoid(gate) * up).astype(BF16)
    out[...] = jnp.broadcast_to(hidden[None], out.shape)


def close(resid, got, out):
    total = resid[...] + jnp.sum(got[...], 0)
    out[...] = total.astype(BF16).reshape(out.shape)


def shards(
    tokens,
    norm_attn,
    norm_ffn,
    w_query,
    w_kv,
    w_out,
    w_gate_up,
    w_down,
    cache_keys,
    cache_values,
    lengths,
    owner,
):
    kv_index = lax.axis_index("kv").astype(jnp.int32)
    kv_count = lax.axis_size("kv")
    head_count = lax.axis_size("head")
    steps, rollouts, width = tokens.shape
    rows = steps * rollouts
    span, hd = cache_keys.shape[2:]
    shape = jax.ShapeDtypeStruct
    w_gate_up = w_gate_up.transpose(1, 0, 2)

    chunk = call(
        project,
        shape((kv_count * 8, hd), F32),
        (tokens, norm_attn, w_query, w_kv),
        [ANY] * 4,
        [pltpu.VMEM(x.shape, x.dtype) for x in (tokens, norm_attn, w_query, w_kv)]
        + [pltpu.VMEM((2 * width, hd), F32), pltpu.SemaphoreType.DMA((4,))],
        60,
    )
    got = exchange(chunk.reshape(kv_count, 8, hd), "kv")
    mine = call(
        finish, shape((kv_count, 8, hd), BF16), (got, w_gate_up), [VMEM, ANY], limit=60
    )
    whole = exchange(mine, "kv")

    cache_shape = (rollouts, span, hd)
    keys, values = cache_keys.reshape(cache_shape), cache_values.reshape(cache_shape)
    chunk, stored = call(
        attend,
        (shape((kv_count, 8, hd), F32), shape((1, steps, rollouts, 1, 2, hd), BF16)),
        (lengths, owner, kv_index.reshape(1), whole, keys, values),
        [SMEM, SMEM, SMEM, VMEM, VMEM, VMEM],
    )
    got = exchange(chunk, "kv")
    context = exchange(call(combine, shape((kv_count, 4, hd), BF16), (got,)), "kv")
    part = call(
        functools.partial(gathered_dot, 4),
        shape((head_count, rows, width), F32),
        (context, w_out),
        scratch=[pltpu.VMEM((kv_count * 4, hd), F32)],
    )
    got = exchange(part, "head")

    resid, chunk = call(
        gate_up,
        (shape((rows, width), F32), shape((kv_count * 32, hd), F32)),
        (got, tokens, norm_ffn, w_gate_up),
    )
    got = exchange(chunk.reshape(kv_count, 32, hd), "kv")
    hidden = exchange(call(activate, shape((kv_count, 16, hd), BF16), (got,)), "kv")
    part = call(
        functools.partial(gathered_dot, w_down.shape[0] // 2 // hd),
        shape((head_count, rows, width), F32),
        (hidden, w_down),
        scratch=[pltpu.VMEM((kv_count * 16, hd), F32)],
    )
    got = exchange(part, "head")
    layer_out = call(close, shape((steps, rollouts, width), BF16), (resid, got))
    return (layer_out, stored)


def solution(mesh):
    return jax.shard_map(
        shards,
        mesh=mesh,
        in_specs=(
            P(None, None, "kv"),
            P("kv"),
            P("kv"),
            P("kv", "head"),
            P("kv", None, "head"),
            P("head", "kv"),
            P("kv", None, "head"),
            P("head", "kv"),
            P(None, "head", "kv", None),
            P(None, "head", "kv", None),
            P(),
            P(),
        ),
        out_specs=(P(None, None, "kv"), P("kv", None, None, "head", None, None)),
        check_vma=False,
    )
```

```python
import functools

import jax
import jax.numpy as jnp
from jax import lax
from jax.experimental import pallas as pl
from jax.experimental.pallas import tpu as pltpu
from jax.sharding import PartitionSpec as P

D = 8192
EPSILON = 1e-05
NEGATIVE = -1e30
F32 = jnp.float32
BF16 = jnp.bfloat16
LANES = 128
TOP = 32767.0
VMEM = pl.BlockSpec(memory_space=pltpu.VMEM)
SMEM = pl.BlockSpec(memory_space=pltpu.SMEM)
ANY = pl.BlockSpec(memory_space=pl.ANY)


def exchange(x, axis):
    return lax.all_to_all(x, axis, 0, 0, tiled=True)


def call(body, out_shape, args, specs=None, scratch=(), limit=24):
    return pl.pallas_call(
        body,
        out_shape=out_shape,
        in_specs=[VMEM] * len(args) if specs is None else specs,
        out_specs=jax.tree.map(lambda _: VMEM, out_shape),
        scratch_shapes=list(scratch),
        compiler_params=pltpu.CompilerParams(vmem_limit_bytes=int(limit * 2**20)),
    )(*args)


def project(
    index, tokens_at, gain_at, w_query_at, w_kv_at, out, tokens, gain, w_query, w_kv, wide, sems
):
    copies = [
        pltpu.make_async_copy(src, dst, sems.at[i])
        for i, (src, dst) in enumerate(
            ((w_kv_at, w_kv), (tokens_at, tokens), (gain_at, gain), (w_query_at, w_query))
        )
    ]
    for copy in copies:
        copy.start()
    for copy in copies[:3]:
        copy.wait()
    rows = tokens.shape[0] * tokens.shape[1]
    width = tokens.shape[2]
    wide[...] = w_kv[...].astype(F32).reshape(2 * width, LANES)
    flat = tokens[...].astype(F32).reshape(rows, tokens.shape[2])
    normed = (flat * gain[...].astype(F32).reshape(1, -1)).astype(BF16)
    kv = [
        jnp.dot(
            normed, wide[pl.ds(i, width, stride=2), :].astype(BF16), preferred_element_type=F32
        )
        for i in range(2)
    ]
    copies[3].wait()
    q = jnp.dot(normed, w_query[...], preferred_element_type=F32)
    stat = jnp.broadcast_to(jnp.sum(flat * flat, -1, keepdims=True), (rows, LANES))
    for half in range(2):
        for slot in range(8):
            if slot < 4:
                at = (half * 4 + slot) * LANES
                part = q[:, at : at + LANES]
            elif slot == 4:
                part = kv[half]
            else:
                part = stat
            out[pl.ds(half * 8 + slot, rows, stride=16), :] = part


def anchor(relaid, out):
    out[0] = 0


def finish(got, token, values, out):
    total = jnp.sum(got[...], 0)
    inv = lax.rsqrt(total[7:8] / D + EPSILON)
    out[...] = jnp.broadcast_to((total * inv).astype(BF16)[None], out.shape)


def attend(lengths, owner, index, whole, keys, values, out, stored):
    rollouts, span, hd = keys.shape
    scale = hd ** (-0.5)
    row = lax.broadcasted_iota(jnp.int32, (8, LANES), 0)
    lane = lax.broadcasted_iota(jnp.int32, (16, LANES), 1)
    column = lax.broadcasted_iota(jnp.int32, (16, span), 1)
    step = lax.broadcasted_iota(jnp.int32, (16, 1), 0) // 8
    here = index[0] == 0
    queries, news = [], []
    for b in range(rollouts):
        tiles, pairs = [], []
        for s in range(2):
            low = whole[(s * rollouts + b) * 2].astype(F32)
            high = whole[(s * rollouts + b) * 2 + 1].astype(F32)
            tiles.append(jnp.where(row < 4, low, pltpu.roll(high, 4, 0)))
            pairs.append((low[4:5], high[4:5]))
            pair = jnp.concatenate(pairs[s], 0)
            mine = owner[s] == index[0]
            stored[0, s, b, 0] = jnp.where(mine, pair, jnp.zeros_like(pair)).astype(BF16)
        queries.append(jnp.concatenate(tiles, 0))
        news.append(pairs)
    scores = []
    for b in range(rollouts):
        scores.append(
            lax.dot_general(
                queries[b].astype(BF16),
                keys[b],
                (((1,), (1,)), ((), ())),
                preferred_element_type=F32,
            )
            * scale
        )
    weights, totals, tops, extras = [], [], [], []
    for b in range(rollouts):
        keep = column < lengths[b] - index[0] * span
        masked = jnp.where(keep, scores[b], NEGATIVE)
        top = jnp.max(masked, -1, keepdims=True)
        fresh = []
        for t in range(2):
            allowed = (step >= t) & here
            score = jnp.sum(queries[b] * news[b][t][0], -1, keepdims=True) * scale
            fresh.append((allowed, jnp.where(allowed, score, NEGATIVE)))
            top = jnp.maximum(top, fresh[t][1])
        e = jnp.where(keep, jnp.exp(masked - top), 0.0)
        extra = [jnp.where(ok, jnp.exp(score - top), 0.0) for ok, score in fresh]
        totals.append(jnp.sum(e, -1, keepdims=True) + extra[0] + extra[1])
        weights.append(e.astype(BF16))
        tops.append(top)
        extras.append(extra)
    for b in range(rollouts):
        sums = jnp.dot(weights[b], values[b], preferred_element_type=F32)
        for t in range(2):
            sums = sums + extras[b][t].astype(BF16).astype(F32) * news[b][t][1]
        stat = jnp.where(lane < LANES // 2, tops[b], totals[b])
        for s in range(2):
            sums_s, stat_s = sums[s * 8 : s * 8 + 8], stat[s * 8 : s * 8 + 8]
            at = (s * rollouts + b) * 2
            out[at] = jnp.where(row < 4, sums_s, pltpu.roll(stat_s, 4, 0))
            out[at + 1] = jnp.where(row < 4, pltpu.roll(sums_s, 4, 0), stat_s)


def combine(got, out):
    tops = got[:, 4:, :1]
    factor = jnp.exp(tops - jnp.max(tops, 0, keepdims=True))
    total = jnp.sum(factor * got[:, 4:, LANES // 2 : LANES // 2 + 1], 0)
    context = jnp.sum(factor * got[:, :4, :], 0) / total
    out[...] = jnp.broadcast_to(context.astype(BF16)[None], out.shape)


def gathered_dot(used, whole, w, out, wide):
    chunks, lines = whole.shape[:2]
    wide[...] = whole[...].astype(F32).reshape(chunks * lines, LANES)
    rows = chunks // 2
    parts = [
        wide[pl.ds(half * lines + slot, rows, stride=2 * lines), :].astype(BF16)
        for half in range(2)
        for slot in range(used)
    ]
    part = jnp.dot(jnp.concatenate(parts, 1), w[...], preferred_element_type=F32)
    out[...] = jnp.broadcast_to(part[None], out.shape)


def exponent(x):
    return jnp.ceil(jnp.log2(jnp.maximum(x, 1e-30)))


def gate_up(got, tokens, gain, w, resid_out, out, wide):
    rows, width = resid_out.shape
    resid = tokens[...].astype(F32).reshape(rows, width) + jnp.sum(got[...], 0)
    resid_out[...] = resid
    normed = (resid * gain[...].astype(F32).reshape(1, -1)).astype(BF16)
    stat = jnp.sum(resid * resid, -1, keepdims=True)
    power = exponent(stat)
    scaled = stat * jnp.exp2(-power) * TOP
    high = jnp.floor(scaled)
    low = jnp.floor((scaled - high) * TOP)
    lines = w.shape[2] // 2 // LANES
    across = lines * LANES
    parts = [jnp.dot(normed, w[which], preferred_element_type=F32) for which in range(2)]
    for half in range(2):
        pair = [part[:, half * across : (half + 1) * across] for part in parts]
        size = jnp.maximum(*(jnp.max(jnp.abs(part), -1, keepdims=True) for part in pair))
        shift = exponent(size)
        factor = jnp.exp2(-shift) * TOP
        extras = ((shift, high), (low, power))
        for which in range(2):
            for slot in range(16):
                if slot < lines:
                    line = jnp.floor(
                        pair[which][:, slot * LANES : (slot + 1) * LANES] * factor + 0.5
                    )
                    line = jnp.clip(line, -TOP, TOP)
                else:
                    line = jnp.broadcast_to(extras[which][slot - lines], (rows, LANES))
                wide[pl.ds(half * 32 + which * 16 + slot, rows, stride=64), :] = line
    out[...] = wide[...].astype(jnp.int32).astype(jnp.int16).reshape(out.shape)


def activate(got, out):
    coded = got[...].astype(jnp.int32).astype(F32)
    total = jnp.sum(coded * (jnp.exp2(coded[:, 14:15]) / TOP), 0)
    stats = (coded[:, 15:16] + coded[:, 30:31] / TOP) * (jnp.exp2(coded[:, 31:32]) / TOP)
    inv = lax.rsqrt(jnp.sum(stats, 0) / D + EPSILON)
    gate, up = total[:16] * inv, total[16:] * inv
    hidden = (gate * jax.nn.sigmoid(gate) * up).astype(BF16)
    out[...] = jnp.broadcast_to(hidden[None], out.shape)


def close(resid, got, out):
    total = resid[...] + jnp.sum(got[...], 0)
    out[...] = total.astype(BF16).reshape(out.shape)


def shards(
    tokens,
    norm_attn,
    norm_ffn,
    w_query,
    w_kv,
    w_out,
    w_gate_up,
    w_down,
    cache_keys,
    cache_values,
    lengths,
    owner,
):
    kv_index = lax.axis_index("kv").astype(jnp.int32)
    kv_count = lax.axis_size("kv")
    head_count = lax.axis_size("head")
    steps, rollouts, width = tokens.shape
    rows = steps * rollouts
    span, hd = cache_keys.shape[2:]
    shape = jax.ShapeDtypeStruct
    w_gate_up = w_gate_up.transpose(1, 0, 2)

    chunk = call(
        project,
        shape((kv_count * 8, hd), F32),
        (kv_index.reshape(1), tokens, norm_attn, w_query, w_kv),
        [SMEM] + [ANY] * 4,
        [pltpu.VMEM(x.shape, x.dtype) for x in (tokens, norm_attn, w_query, w_kv)]
        + [pltpu.VMEM((2 * width, hd), F32), pltpu.SemaphoreType.DMA((4,))],
        60,
    )
    got = exchange(chunk.reshape(kv_count, 8, hd), "kv")
    token = pl.pallas_call(
        anchor,
        out_shape=shape((1,), jnp.int32),
        in_specs=[ANY],
        out_specs=SMEM,
        compiler_params=pltpu.CompilerParams(vmem_limit_bytes=61 * 2**20),
    )(w_gate_up)
    cache_shape = (rollouts, span, hd)
    keys, values = cache_keys.reshape(cache_shape), cache_values.reshape(cache_shape)
    mine = call(
        finish, shape((kv_count, 8, hd), BF16), (got, token, values), [VMEM, SMEM, VMEM]
    )
    whole = exchange(mine, "kv")

    chunk, stored = call(
        attend,
        (shape((kv_count, 8, hd), F32), shape((1, steps, rollouts, 1, 2, hd), BF16)),
        (lengths, owner, kv_index.reshape(1), whole, keys, values),
        [SMEM, SMEM, SMEM, VMEM, VMEM, VMEM],
    )
    got = exchange(chunk, "kv")
    context = exchange(call(combine, shape((kv_count, 4, hd), BF16), (got,)), "kv")
    part = call(
        functools.partial(gathered_dot, 4),
        shape((head_count, rows, width), F32),
        (context, w_out),
        scratch=[pltpu.VMEM((kv_count * 4, hd), F32)],
    )
    got = exchange(part, "head")

    resid, chunk = call(
        gate_up,
        (shape((rows, width), F32), shape((kv_count, 32, hd), jnp.int16)),
        (got, tokens, norm_ffn, w_gate_up),
        scratch=[pltpu.VMEM((kv_count * 32, hd), F32)],
    )
    got = exchange(chunk, "kv")
    hidden = exchange(call(activate, shape((kv_count, 16, hd), BF16), (got,)), "kv")
    part = call(
        functools.partial(gathered_dot, w_down.shape[0] // 2 // hd),
        shape((head_count, rows, width), F32),
        (hidden, w_down),
        scratch=[pltpu.VMEM((kv_count * 16, hd), F32)],
    )
    got = exchange(part, "head")
    layer_out = call(close, shape((steps, rollouts, width), BF16), (resid, got))
    return (layer_out, stored)


def solution(mesh):
    return jax.shard_map(
        shards,
        mesh=mesh,
        in_specs=(
            P(None, None, "kv"),
            P("kv"),
            P("kv"),
            P("kv", "head"),
            P("kv", None, "head"),
            P("head", "kv"),
            P("kv", None, "head"),
            P("head", "kv"),
            P(None, "head", "kv", None),
            P(None, "head", "kv", None),
            P(),
            P(),
        ),
        out_specs=(P(None, None, "kv"), P("kv", None, None, "head", None, None)),
        check_vma=False,
    )
```

```python
import functools

import jax
import jax.numpy as jnp
from jax import lax
from jax.experimental import pallas as pl
from jax.experimental.pallas import tpu as pltpu
from jax.sharding import PartitionSpec as P

D = 8192
EPSILON = 1e-05
NEGATIVE = -1e30
F32 = jnp.float32
BF16 = jnp.bfloat16
LANES = 128
TOP = 32767.0
VMEM = pl.BlockSpec(memory_space=pltpu.VMEM)
ANY = pl.BlockSpec(memory_space=pl.ANY)


def ring(sizes, first):
    major, minor = sizes
    return [
        (a + first[0]) % major * minor + (b + first[1]) % minor
        for a in range(major)
        for b in range(minor)
    ]


ORDER = {"kv": ring((8, 4), (4, 2)), "head": ring((4, 2), (2, 0))}


def exchange(x, axis):
    return lax.all_to_all(x, axis, 0, 0, tiled=True, axis_index_groups=[ORDER[axis]])


def call(body, out_shape, args, specs=None, scratch=(), limit=24):
    return pl.pallas_call(
        body,
        out_shape=out_shape,
        in_specs=[VMEM] * len(args) if specs is None else specs,
        out_specs=jax.tree.map(lambda _: VMEM, out_shape),
        scratch_shapes=list(scratch),
        compiler_params=pltpu.CompilerParams(vmem_limit_bytes=int(limit * 2**20)),
    )(*args)


def project(
    tokens_at, gain_at, w_query_at, w_kv_at, out, tokens, gain, w_query, w_kv, wide, sems
):
    copies = [
        pltpu.make_async_copy(src, dst, sems.at[i])
        for i, (src, dst) in enumerate(
            ((w_kv_at, w_kv), (tokens_at, tokens), (gain_at, gain), (w_query_at, w_query))
        )
    ]
    for copy in copies:
        copy.start()
    for copy in copies[:3]:
        copy.wait()
    rows = tokens.shape[0] * tokens.shape[1]
    width = tokens.shape[2]
    wide[...] = w_kv[...].astype(F32).reshape(2 * width, LANES)
    flat = tokens[...].astype(F32).reshape(rows, tokens.shape[2])
    normed = (flat * gain[...].astype(F32).reshape(1, -1)).astype(BF16)
    kv = [
        jnp.dot(
            normed, wide[pl.ds(i, width, stride=2), :].astype(BF16), preferred_element_type=F32
        )
        for i in range(2)
    ]
    copies[3].wait()
    q = jnp.dot(normed, w_query[...], preferred_element_type=F32)
    stat = jnp.broadcast_to(jnp.sum(flat * flat, -1, keepdims=True), (rows, LANES))
    for half in range(2):
        for slot in range(8):
            if slot < 4:
                at = (half * 4 + slot) * LANES
                part = q[:, at : at + LANES]
            elif slot == 4:
                part = kv[half]
            else:
                part = stat
            out[pl.ds(half * 8 + slot, rows, stride=16), :] = part


def finish(got, relaid, values, out):
    total = jnp.sum(got[...], 0)
    inv = lax.rsqrt(total[7:8] / D + EPSILON)
    out[...] = jnp.broadcast_to((total * inv).astype(BF16)[None], out.shape)


def attend(lengths, owner, whole, keys, values, out, stored):
    rollouts, span, hd = keys.shape
    index = lax.axis_index("kv")
    live = lengths[...].reshape(1, rollouts) - index * span
    holder = owner[...].reshape(1, 2) == index
    scale = hd ** (-0.5)
    row = lax.broadcasted_iota(jnp.int32, (8, LANES), 0)
    lane = lax.broadcasted_iota(jnp.int32, (16, LANES), 1)
    column = lax.broadcasted_iota(jnp.int32, (16, span), 1)
    step = lax.broadcasted_iota(jnp.int32, (16, 1), 0) // 8
    here = index == 0
    queries, news = [], []
    for b in range(rollouts):
        tiles, pairs = [], []
        for s in range(2):
            low = whole[(s * rollouts + b) * 2].astype(F32)
            high = whole[(s * rollouts + b) * 2 + 1].astype(F32)
            tiles.append(jnp.where(row < 4, low, pltpu.roll(high, 4, 0)))
            pairs.append((low[4:5], high[4:5]))
            pair = jnp.concatenate(pairs[s], 0)
            mine = holder[:, s : s + 1]
            stored[0, s, b, 0] = jnp.where(mine, pair, jnp.zeros_like(pair)).astype(BF16)
        queries.append(jnp.concatenate(tiles, 0))
        news.append(pairs)
    scores = []
    for b in range(rollouts):
        scores.append(
            lax.dot_general(
                queries[b].astype(BF16),
                keys[b],
                (((1,), (1,)), ((), ())),
                preferred_element_type=F32,
            )
            * scale
        )
    weights, totals, tops, extras = [], [], [], []
    for b in range(rollouts):
        keep = column < live[:, b : b + 1]
        masked = jnp.where(keep, scores[b], NEGATIVE)
        top = jnp.max(masked, -1, keepdims=True)
        fresh = []
        for t in range(2):
            allowed = (step >= t) & here
            score = jnp.sum(queries[b] * news[b][t][0], -1, keepdims=True) * scale
            fresh.append((allowed, jnp.where(allowed, score, NEGATIVE)))
            top = jnp.maximum(top, fresh[t][1])
        e = jnp.where(keep, jnp.exp(masked - top), 0.0)
        extra = [jnp.where(ok, jnp.exp(score - top), 0.0) for ok, score in fresh]
        totals.append(jnp.sum(e, -1, keepdims=True) + extra[0] + extra[1])
        weights.append(e.astype(BF16))
        tops.append(top)
        extras.append(extra)
    for b in range(rollouts):
        sums = jnp.dot(weights[b], values[b], preferred_element_type=F32)
        for t in range(2):
            sums = sums + extras[b][t].astype(BF16).astype(F32) * news[b][t][1]
        stat = jnp.where(lane < LANES // 2, tops[b], totals[b])
        for s in range(2):
            sums_s, stat_s = sums[s * 8 : s * 8 + 8], stat[s * 8 : s * 8 + 8]
            at = (s * rollouts + b) * 2
            out[at] = jnp.where(row < 4, sums_s, pltpu.roll(stat_s, 4, 0))
            out[at + 1] = jnp.where(row < 4, pltpu.roll(sums_s, 4, 0), stat_s)


def combine(got, out):
    tops = got[:, 4:, :1]
    factor = jnp.exp(tops - jnp.max(tops, 0, keepdims=True))
    total = jnp.sum(factor * got[:, 4:, LANES // 2 : LANES // 2 + 1], 0)
    context = jnp.sum(factor * got[:, :4, :], 0) / total
    out[...] = jnp.broadcast_to(context.astype(BF16)[None], out.shape)


def gathered_dot(used, whole, w, out, wide):
    chunks, lines = whole.shape[:2]
    wide[...] = whole[...].astype(F32).reshape(chunks * lines, LANES)
    rows = chunks // 2
    parts = [
        wide[pl.ds(half * lines + slot, rows, stride=2 * lines), :].astype(BF16)
        for half in range(2)
        for slot in range(used)
    ]
    part = jnp.dot(jnp.concatenate(parts, 1), w[...], preferred_element_type=F32)
    out[...] = jnp.broadcast_to(part[None], out.shape)


def exponent(x):
    return jnp.ceil(jnp.log2(jnp.maximum(x, 1e-30)))


def gate_up(got, tokens, gain, w, resid_out, out, wide):
    rows, width = resid_out.shape
    resid = tokens[...].astype(F32).reshape(rows, width) + jnp.sum(got[...], 0)
    resid_out[...] = resid
    normed = (resid * gain[...].astype(F32).reshape(1, -1)).astype(BF16)
    stat = jnp.sum(resid * resid, -1, keepdims=True)
    power = exponent(stat)
    scaled = stat * jnp.exp2(-power) * TOP
    high = jnp.floor(scaled)
    low = jnp.floor((scaled - high) * TOP)
    lines = w.shape[2] // 2 // LANES
    across = lines * LANES
    parts = [jnp.dot(normed, w[which], preferred_element_type=F32) for which in range(2)]
    for half in range(2):
        pair = [part[:, half * across : (half + 1) * across] for part in parts]
        size = jnp.maximum(*(jnp.max(jnp.abs(part), -1, keepdims=True) for part in pair))
        shift = exponent(size)
        factor = jnp.exp2(-shift) * TOP
        extras = ((shift, high), (low, power))
        for which in range(2):
            for slot in range(16):
                if slot < lines:
                    line = jnp.floor(
                        pair[which][:, slot * LANES : (slot + 1) * LANES] * factor + 0.5
                    )
                    line = jnp.clip(line, -TOP, TOP)
                else:
                    line = jnp.broadcast_to(extras[which][slot - lines], (rows, LANES))
                wide[pl.ds(half * 32 + which * 16 + slot, rows, stride=64), :] = line
    out[...] = wide[...].astype(jnp.int32).astype(jnp.int16).reshape(out.shape)


def activate(got, out):
    coded = got[...].astype(jnp.int32).astype(F32)
    total = jnp.sum(coded * (jnp.exp2(coded[:, 14:15]) / TOP), 0)
    stats = (coded[:, 15:16] + coded[:, 30:31] / TOP) * (jnp.exp2(coded[:, 31:32]) / TOP)
    inv = lax.rsqrt(jnp.sum(stats, 0) / D + EPSILON)
    gate, up = total[:16] * inv, total[16:] * inv
    hidden = (gate * jax.nn.sigmoid(gate) * up).astype(BF16)
    out[...] = jnp.broadcast_to(hidden[None], out.shape)


def close(resid, got, out):
    total = resid[...] + jnp.sum(got[...], 0)
    out[...] = total.astype(BF16).reshape(out.shape)


def shards(
    tokens,
    norm_attn,
    norm_ffn,
    w_query,
    w_kv,
    w_out,
    w_gate_up,
    w_down,
    cache_keys,
    cache_values,
    lengths,
    owner,
):
    kv_count = lax.axis_size("kv")
    head_count = lax.axis_size("head")
    steps, rollouts, width = tokens.shape
    rows = steps * rollouts
    span, hd = cache_keys.shape[2:]
    shape = jax.ShapeDtypeStruct
    w_gate_up = w_gate_up.transpose(1, 0, 2)

    chunk = call(
        project,
        shape((kv_count * 8, hd), F32),
        (tokens, norm_attn, w_query, w_kv),
        [ANY] * 4,
        [pltpu.VMEM(x.shape, x.dtype) for x in (tokens, norm_attn, w_query, w_kv)]
        + [pltpu.VMEM((2 * width, hd), F32), pltpu.SemaphoreType.DMA((4,))],
        60,
    )
    got = exchange(chunk.reshape(kv_count, 8, hd), "kv")
    cache_shape = (rollouts, span, hd)
    keys, values = cache_keys.reshape(cache_shape), cache_values.reshape(cache_shape)
    mine = call(
        finish,
        shape((kv_count, 8, hd), BF16),
        (got, w_gate_up, values),
        [VMEM, ANY, VMEM],
        limit=51,
    )
    whole = exchange(mine, "kv")

    chunk, stored = call(
        attend,
        (shape((kv_count, 8, hd), F32), shape((1, steps, rollouts, 1, 2, hd), BF16)),
        (lengths, owner, whole, keys, values),
        [VMEM] * 5,
    )
    got = exchange(chunk, "kv")
    context = exchange(call(combine, shape((kv_count, 4, hd), BF16), (got,)), "kv")
    part = call(
        functools.partial(gathered_dot, 4),
        shape((head_count, rows, width), F32),
        (context, w_out),
        scratch=[pltpu.VMEM((kv_count * 4, hd), F32)],
    )
    got = exchange(part, "head")

    resid, chunk = call(
        gate_up,
        (shape((rows, width), F32), shape((kv_count, 32, hd), jnp.int16)),
        (got, tokens, norm_ffn, w_gate_up),
        scratch=[pltpu.VMEM((kv_count * 32, hd), F32)],
    )
    got = exchange(chunk, "kv")
    hidden = exchange(call(activate, shape((kv_count, 16, hd), BF16), (got,)), "kv")
    part = call(
        functools.partial(gathered_dot, w_down.shape[0] // 2 // hd),
        shape((head_count, rows, width), F32),
        (hidden, w_down),
        scratch=[pltpu.VMEM((kv_count * 16, hd), F32)],
    )
    got = exchange(part, "head")
    layer_out = call(close, shape((steps, rollouts, width), BF16), (resid, got))
    return (layer_out, stored)


def solution(mesh):
    return jax.shard_map(
        shards,
        mesh=mesh,
        in_specs=(
            P(None, None, "kv"),
            P("kv"),
            P("kv"),
            P("kv", "head"),
            P("kv", None, "head"),
            P("head", "kv"),
            P("kv", None, "head"),
            P("head", "kv"),
            P(None, "head", "kv", None),
            P(None, "head", "kv", None),
            P(),
            P(),
        ),
        out_specs=(P(None, None, "kv"), P("kv", None, None, "head", None, None)),
        check_vma=False,
    )
```

```python
import functools

import jax
import jax.numpy as jnp
from jax import lax
from jax.experimental import pallas as pl
from jax.experimental.pallas import tpu as pltpu
from jax.sharding import PartitionSpec as P

D = 8192
EPSILON = 1e-05
NEGATIVE = -1e30
F32 = jnp.float32
BF16 = jnp.bfloat16
LANES = 128
TOP = 32767.0
VMEM = pl.BlockSpec(memory_space=pltpu.VMEM)
ANY = pl.BlockSpec(memory_space=pl.ANY)


def ring(sizes, first):
    major, minor = sizes
    return [
        (a + first[0]) % major * minor + (b + first[1]) % minor
        for a in range(major)
        for b in range(minor)
    ]


SCATTER, GATHER, HEAD = ring((8, 4), (5, 2)), ring((8, 4), (4, 2)), ring((4, 2), (2, 0))
TURN = 4


def exchange(x, axis, order):
    return lax.all_to_all(x, axis, 0, 0, tiled=True, axis_index_groups=[order])


def call(body, out_shape, args, specs=None, scratch=(), limit=24):
    return pl.pallas_call(
        body,
        out_shape=out_shape,
        in_specs=[VMEM] * len(args) if specs is None else specs,
        out_specs=jax.tree.map(lambda _: VMEM, out_shape),
        scratch_shapes=list(scratch),
        compiler_params=pltpu.CompilerParams(vmem_limit_bytes=int(limit * 2**20)),
    )(*args)


def project(
    tokens_at, gain_at, w_query_at, w_kv_at, out, tokens, gain, w_query, w_kv, wide, sems
):
    copies = [
        pltpu.make_async_copy(src, dst, sems.at[i])
        for i, (src, dst) in enumerate(
            ((w_kv_at, w_kv), (tokens_at, tokens), (gain_at, gain), (w_query_at, w_query))
        )
    ]
    for copy in copies:
        copy.start()
    for copy in copies[:3]:
        copy.wait()
    rows = tokens.shape[0] * tokens.shape[1]
    width = tokens.shape[2]
    wide[...] = w_kv[...].astype(F32).reshape(2 * width, LANES)
    flat = tokens[...].astype(F32).reshape(rows, tokens.shape[2])
    normed = (flat * gain[...].astype(F32).reshape(1, -1)).astype(BF16)
    kv = [
        jnp.dot(
            normed, wide[pl.ds(i, width, stride=2), :].astype(BF16), preferred_element_type=F32
        )
        for i in range(2)
    ]
    copies[3].wait()
    q = jnp.dot(normed, w_query[...], preferred_element_type=F32)
    stat = jnp.broadcast_to(jnp.sum(flat * flat, -1, keepdims=True), (rows, LANES))
    for half in range(2):
        for slot in range(8):
            if slot < 4:
                at = (half * 4 + slot) * LANES
                part = q[:, at : at + LANES]
            elif slot == 4:
                part = kv[half]
            else:
                part = stat
            out[pl.ds(half * 8 + slot, rows, stride=16), :] = part


def finish(got, relaid, values, out):
    total = jnp.sum(got[...], 0)
    inv = lax.rsqrt(total[7:8] / D + EPSILON)
    out[...] = jnp.broadcast_to((total * inv).astype(BF16)[None], out.shape)


def attend(lengths, owner, whole, keys, values, out, stored):
    rollouts, span, hd = keys.shape
    index = lax.axis_index("kv")
    live = lengths[...].reshape(1, rollouts) - index * span
    holder = owner[...].reshape(1, 2) == index
    scale = hd ** (-0.5)
    row = lax.broadcasted_iota(jnp.int32, (8, LANES), 0)
    lane = lax.broadcasted_iota(jnp.int32, (16, LANES), 1)
    column = lax.broadcasted_iota(jnp.int32, (16, span), 1)
    step = lax.broadcasted_iota(jnp.int32, (16, 1), 0) // 8
    here = index == 0
    queries, news = [], []
    for b in range(rollouts):
        tiles, pairs = [], []
        for s in range(2):
            at = ((s * rollouts + b) * 2 + TURN) % whole.shape[0]
            low = whole[at].astype(F32)
            high = whole[at + 1].astype(F32)
            tiles.append(jnp.where(row < 4, low, pltpu.roll(high, 4, 0)))
            pairs.append((low[4:5], high[4:5]))
            pair = jnp.concatenate(pairs[s], 0)
            mine = holder[:, s : s + 1]
            stored[0, s, b, 0] = jnp.where(mine, pair, jnp.zeros_like(pair)).astype(BF16)
        queries.append(jnp.concatenate(tiles, 0))
        news.append(pairs)
    scores = []
    for b in range(rollouts):
        scores.append(
            lax.dot_general(
                queries[b].astype(BF16),
                keys[b],
                (((1,), (1,)), ((), ())),
                preferred_element_type=F32,
            )
            * scale
        )
    weights, totals, tops, extras = [], [], [], []
    for b in range(rollouts):
        keep = column < live[:, b : b + 1]
        masked = jnp.where(keep, scores[b], NEGATIVE)
        top = jnp.max(masked, -1, keepdims=True)
        fresh = []
        for t in range(2):
            allowed = (step >= t) & here
            score = jnp.sum(queries[b] * news[b][t][0], -1, keepdims=True) * scale
            fresh.append((allowed, jnp.where(allowed, score, NEGATIVE)))
            top = jnp.maximum(top, fresh[t][1])
        e = jnp.where(keep, jnp.exp(masked - top), 0.0)
        extra = [jnp.where(ok, jnp.exp(score - top), 0.0) for ok, score in fresh]
        totals.append(jnp.sum(e, -1, keepdims=True) + extra[0] + extra[1])
        weights.append(e.astype(BF16))
        tops.append(top)
        extras.append(extra)
    for b in range(rollouts):
        sums = jnp.dot(weights[b], values[b], preferred_element_type=F32)
        for t in range(2):
            sums = sums + extras[b][t].astype(BF16).astype(F32) * news[b][t][1]
        stat = jnp.where(lane < LANES // 2, tops[b], totals[b])
        for s in range(2):
            sums_s, stat_s = sums[s * 8 : s * 8 + 8], stat[s * 8 : s * 8 + 8]
            at = (s * rollouts + b) * 2
            out[at] = jnp.where(row < 4, sums_s, pltpu.roll(stat_s, 4, 0))
            out[at + 1] = jnp.where(row < 4, pltpu.roll(sums_s, 4, 0), stat_s)


def combine(got, out):
    tops = got[:, 4:, :1]
    factor = jnp.exp(tops - jnp.max(tops, 0, keepdims=True))
    total = jnp.sum(factor * got[:, 4:, LANES // 2 : LANES // 2 + 1], 0)
    context = jnp.sum(factor * got[:, :4, :], 0) / total
    out[...] = jnp.broadcast_to(context.astype(BF16)[None], out.shape)


def gathered_dot(used, whole, w, out, wide):
    chunks, lines = whole.shape[:2]
    wide[...] = whole[...].astype(F32).reshape(chunks * lines, LANES)
    rows = chunks // 2
    parts = [
        wide[pl.ds(half * lines + slot, rows, stride=2 * lines), :].astype(BF16)
        for half in range(2)
        for slot in range(used)
    ]
    part = jnp.dot(jnp.concatenate(parts, 1), w[...], preferred_element_type=F32)
    part = jnp.concatenate([part[TURN // 2 :], part[: TURN // 2]], 0)
    out[...] = jnp.broadcast_to(part[None], out.shape)


def exponent(x):
    return jnp.ceil(jnp.log2(jnp.maximum(x, 1e-30)))


def gate_up(got, tokens, gain, w, resid_out, out, wide):
    rows, width = resid_out.shape
    resid = tokens[...].astype(F32).reshape(rows, width) + jnp.sum(got[...], 0)
    resid_out[...] = resid
    normed = (resid * gain[...].astype(F32).reshape(1, -1)).astype(BF16)
    stat = jnp.sum(resid * resid, -1, keepdims=True)
    power = exponent(stat)
    scaled = stat * jnp.exp2(-power) * TOP
    high = jnp.floor(scaled)
    low = jnp.floor((scaled - high) * TOP)
    lines = w.shape[2] // 2 // LANES
    across = lines * LANES
    parts = [jnp.dot(normed, w[which], preferred_element_type=F32) for which in range(2)]
    for half in range(2):
        pair = [part[:, half * across : (half + 1) * across] for part in parts]
        size = jnp.maximum(*(jnp.max(jnp.abs(part), -1, keepdims=True) for part in pair))
        shift = exponent(size)
        factor = jnp.exp2(-shift) * TOP
        extras = ((shift, high), (low, power))
        for which in range(2):
            for slot in range(16):
                if slot < lines:
                    line = jnp.floor(
                        pair[which][:, slot * LANES : (slot + 1) * LANES] * factor + 0.5
                    )
                    line = jnp.clip(line, -TOP, TOP)
                else:
                    line = jnp.broadcast_to(extras[which][slot - lines], (rows, LANES))
                wide[pl.ds(half * 32 + which * 16 + slot, rows, stride=64), :] = line
    out[...] = wide[...].astype(jnp.int32).astype(jnp.int16).reshape(out.shape)


def activate(got, out):
    coded = got[...].astype(jnp.int32).astype(F32)
    total = jnp.sum(coded * (jnp.exp2(coded[:, 14:15]) / TOP), 0)
    stats = (coded[:, 15:16] + coded[:, 30:31] / TOP) * (jnp.exp2(coded[:, 31:32]) / TOP)
    inv = lax.rsqrt(jnp.sum(stats, 0) / D + EPSILON)
    gate, up = total[:16] * inv, total[16:] * inv
    hidden = (gate * jax.nn.sigmoid(gate) * up).astype(BF16)
    out[...] = jnp.broadcast_to(hidden[None], out.shape)


def close(resid, got, out):
    total = resid[...] + jnp.sum(got[...], 0)
    out[...] = total.astype(BF16).reshape(out.shape)


def shards(
    tokens,
    norm_attn,
    norm_ffn,
    w_query,
    w_kv,
    w_out,
    w_gate_up,
    w_down,
    cache_keys,
    cache_values,
    lengths,
    owner,
):
    kv_count = lax.axis_size("kv")
    head_count = lax.axis_size("head")
    steps, rollouts, width = tokens.shape
    rows = steps * rollouts
    span, hd = cache_keys.shape[2:]
    shape = jax.ShapeDtypeStruct
    w_gate_up = w_gate_up.transpose(1, 0, 2)

    chunk = call(
        project,
        shape((kv_count * 8, hd), F32),
        (tokens, norm_attn, w_query, w_kv),
        [ANY] * 4,
        [pltpu.VMEM(x.shape, x.dtype) for x in (tokens, norm_attn, w_query, w_kv)]
        + [pltpu.VMEM((2 * width, hd), F32), pltpu.SemaphoreType.DMA((4,))],
        60,
    )
    got = exchange(chunk.reshape(kv_count, 8, hd), "kv", SCATTER)
    cache_shape = (rollouts, span, hd)
    keys, values = cache_keys.reshape(cache_shape), cache_values.reshape(cache_shape)
    mine = call(
        finish,
        shape((kv_count, 8, hd), BF16),
        (got, w_gate_up, values),
        [VMEM, ANY, VMEM],
        limit=51,
    )
    whole = exchange(mine, "kv", GATHER)

    chunk, stored = call(
        attend,
        (shape((kv_count, 8, hd), F32), shape((1, steps, rollouts, 1, 2, hd), BF16)),
        (lengths, owner, whole, keys, values),
        [VMEM] * 5,
    )
    got = exchange(chunk, "kv", SCATTER)
    context = exchange(call(combine, shape((kv_count, 4, hd), BF16), (got,)), "kv", GATHER)
    part = call(
        functools.partial(gathered_dot, 4),
        shape((head_count, rows, width), F32),
        (context, w_out),
        scratch=[pltpu.VMEM((kv_count * 4, hd), F32)],
    )
    got = exchange(part, "head", HEAD)

    resid, chunk = call(
        gate_up,
        (shape((rows, width), F32), shape((kv_count, 32, hd), jnp.int16)),
        (got, tokens, norm_ffn, w_gate_up),
        scratch=[pltpu.VMEM((kv_count * 32, hd), F32)],
    )
    got = exchange(chunk, "kv", SCATTER)
    hidden = exchange(call(activate, shape((kv_count, 16, hd), BF16), (got,)), "kv", GATHER)
    part = call(
        functools.partial(gathered_dot, w_down.shape[0] // 2 // hd),
        shape((head_count, rows, width), F32),
        (hidden, w_down),
        scratch=[pltpu.VMEM((kv_count * 16, hd), F32)],
    )
    got = exchange(part, "head", HEAD)
    layer_out = call(close, shape((steps, rollouts, width), BF16), (resid, got))
    return (layer_out, stored)


def solution(mesh):
    return jax.shard_map(
        shards,
        mesh=mesh,
        in_specs=(
            P(None, None, "kv"),
            P("kv"),
            P("kv"),
            P("kv", "head"),
            P("kv", None, "head"),
            P("head", "kv"),
            P("kv", None, "head"),
            P("head", "kv"),
            P(None, "head", "kv", None),
            P(None, "head", "kv", None),
            P(),
            P(),
        ),
        out_specs=(P(None, None, "kv"), P("kv", None, None, "head", None, None)),
        check_vma=False,
    )
```

```python
import functools

import jax
import jax.numpy as jnp
from jax import lax
from jax.experimental import pallas as pl
from jax.experimental.pallas import tpu as pltpu
from jax.sharding import PartitionSpec as P

D = 8192
EPSILON = 1e-05
NEGATIVE = -1e30
F32 = jnp.float32
BF16 = jnp.bfloat16
LANES = 128
TOP = 32767.0
VMEM = pl.BlockSpec(memory_space=pltpu.VMEM)
ANY = pl.BlockSpec(memory_space=pl.ANY)


def by_distance(sizes, first, steps):
    major, minor = sizes

    def distance(index):
        at = (index // minor, index % minor)
        hops = [min((p - q) % n, (q - p) % n) for p, q, n in zip(at, first, sizes)]
        return hops[0] * steps[0] + hops[1] * steps[1]

    return sorted(range(major * minor), key=distance)


SCATTER = by_distance((8, 4), (5, 2), (2, 3))
GATHER = by_distance((8, 4), (5, 2), (2, 3))
HEAD = by_distance((4, 2), (2, 0), (2, 1))
PLACE = [GATHER.index(device) for device in SCATTER]


def exchange(x, axis, order):
    return lax.all_to_all(x, axis, 0, 0, tiled=True, axis_index_groups=[order])


def call(body, out_shape, args, specs=None, scratch=(), limit=24):
    return pl.pallas_call(
        body,
        out_shape=out_shape,
        in_specs=[VMEM] * len(args) if specs is None else specs,
        out_specs=jax.tree.map(lambda _: VMEM, out_shape),
        scratch_shapes=list(scratch),
        compiler_params=pltpu.CompilerParams(vmem_limit_bytes=int(limit * 2**20)),
    )(*args)


def project(
    tokens_at, gain_at, w_query_at, w_kv_at, out, tokens, gain, w_query, w_kv, wide, sems
):
    copies = [
        pltpu.make_async_copy(src, dst, sems.at[i])
        for i, (src, dst) in enumerate(
            ((w_kv_at, w_kv), (tokens_at, tokens), (gain_at, gain), (w_query_at, w_query))
        )
    ]
    for copy in copies:
        copy.start()
    for copy in copies[:3]:
        copy.wait()
    rows = tokens.shape[0] * tokens.shape[1]
    width = tokens.shape[2]
    wide[...] = w_kv[...].astype(F32).reshape(2 * width, LANES)
    flat = tokens[...].astype(F32).reshape(rows, tokens.shape[2])
    normed = (flat * gain[...].astype(F32).reshape(1, -1)).astype(BF16)
    kv = [
        jnp.dot(
            normed, wide[pl.ds(i, width, stride=2), :].astype(BF16), preferred_element_type=F32
        )
        for i in range(2)
    ]
    copies[3].wait()
    q = jnp.dot(normed, w_query[...], preferred_element_type=F32)
    stat = jnp.broadcast_to(jnp.sum(flat * flat, -1, keepdims=True), (rows, LANES))
    for half in range(2):
        for slot in range(8):
            if slot < 4:
                at = (half * 4 + slot) * LANES
                part = q[:, at : at + LANES]
            elif slot == 4:
                part = kv[half]
            else:
                part = stat
            out[pl.ds(half * 8 + slot, rows, stride=16), :] = part


def finish(got, relaid, values, out):
    total = jnp.sum(got[...], 0)
    inv = lax.rsqrt(total[7:8] / D + EPSILON)
    out[...] = jnp.broadcast_to((total * inv).astype(BF16)[None], out.shape)


def attend(lengths, owner, whole, keys, values, out, stored):
    rollouts, span, hd = keys.shape
    index = lax.axis_index("kv")
    live = lengths[...].reshape(1, rollouts) - index * span
    holder = owner[...].reshape(1, 2) == index
    scale = hd ** (-0.5)
    row = lax.broadcasted_iota(jnp.int32, (8, LANES), 0)
    lane = lax.broadcasted_iota(jnp.int32, (16, LANES), 1)
    column = lax.broadcasted_iota(jnp.int32, (16, span), 1)
    step = lax.broadcasted_iota(jnp.int32, (16, 1), 0) // 8
    here = index == 0
    queries, news = [], []
    for b in range(rollouts):
        tiles, pairs = [], []
        for s in range(2):
            at = (s * rollouts + b) * 2
            low = whole[PLACE[at]].astype(F32)
            high = whole[PLACE[at + 1]].astype(F32)
            tiles.append(jnp.where(row < 4, low, pltpu.roll(high, 4, 0)))
            pairs.append((low[4:5], high[4:5]))
            pair = jnp.concatenate(pairs[s], 0)
            mine = holder[:, s : s + 1]
            stored[0, s, b, 0] = jnp.where(mine, pair, jnp.zeros_like(pair)).astype(BF16)
        queries.append(jnp.concatenate(tiles, 0))
        news.append(pairs)
    scores = []
    for b in range(rollouts):
        scores.append(
            lax.dot_general(
                queries[b].astype(BF16),
                keys[b],
                (((1,), (1,)), ((), ())),
                preferred_element_type=F32,
            )
            * scale
        )
    weights, totals, tops, extras = [], [], [], []
    for b in range(rollouts):
        keep = column < live[:, b : b + 1]
        masked = jnp.where(keep, scores[b], NEGATIVE)
        top = jnp.max(masked, -1, keepdims=True)
        fresh = []
        for t in range(2):
            allowed = (step >= t) & here
            score = jnp.sum(queries[b] * news[b][t][0], -1, keepdims=True) * scale
            fresh.append((allowed, jnp.where(allowed, score, NEGATIVE)))
            top = jnp.maximum(top, fresh[t][1])
        e = jnp.where(keep, jnp.exp(masked - top), 0.0)
        extra = [jnp.where(ok, jnp.exp(score - top), 0.0) for ok, score in fresh]
        totals.append(jnp.sum(e, -1, keepdims=True) + extra[0] + extra[1])
        weights.append(e.astype(BF16))
        tops.append(top)
        extras.append(extra)
    for b in range(rollouts):
        sums = jnp.dot(weights[b], values[b], preferred_element_type=F32)
        for t in range(2):
            sums = sums + extras[b][t].astype(BF16).astype(F32) * news[b][t][1]
        stat = jnp.where(lane < LANES // 2, tops[b], totals[b])
        for s in range(2):
            sums_s, stat_s = sums[s * 8 : s * 8 + 8], stat[s * 8 : s * 8 + 8]
            at = (s * rollouts + b) * 2
            out[at] = jnp.where(row < 4, sums_s, pltpu.roll(stat_s, 4, 0))
            out[at + 1] = jnp.where(row < 4, pltpu.roll(sums_s, 4, 0), stat_s)


def combine(got, out):
    tops = got[:, 4:, :1]
    factor = jnp.exp(tops - jnp.max(tops, 0, keepdims=True))
    total = jnp.sum(factor * got[:, 4:, LANES // 2 : LANES // 2 + 1], 0)
    context = jnp.sum(factor * got[:, :4, :], 0) / total
    out[...] = jnp.broadcast_to(context.astype(BF16)[None], out.shape)


def gathered_dot(used, whole, w, out, wide):
    chunks, lines = whole.shape[:2]
    for c in range(chunks):
        wide[c * lines : (c + 1) * lines] = whole[PLACE[c]].astype(F32)
    rows = chunks // 2
    parts = [
        wide[pl.ds(half * lines + slot, rows, stride=2 * lines), :].astype(BF16)
        for half in range(2)
        for slot in range(used)
    ]
    part = jnp.dot(jnp.concatenate(parts, 1), w[...], preferred_element_type=F32)
    out[...] = jnp.broadcast_to(part[None], out.shape)


def exponent(x):
    return jnp.ceil(jnp.log2(jnp.maximum(x, 1e-30)))


def gate_up(got, tokens, gain, w, resid_out, out, wide):
    rows, width = resid_out.shape
    resid = tokens[...].astype(F32).reshape(rows, width) + jnp.sum(got[...], 0)
    resid_out[...] = resid
    normed = (resid * gain[...].astype(F32).reshape(1, -1)).astype(BF16)
    stat = jnp.sum(resid * resid, -1, keepdims=True)
    power = exponent(stat)
    scaled = stat * jnp.exp2(-power) * TOP
    high = jnp.floor(scaled)
    low = jnp.floor((scaled - high) * TOP)
    lines = w.shape[2] // 2 // LANES
    across = lines * LANES
    parts = [jnp.dot(normed, w[which], preferred_element_type=F32) for which in range(2)]
    for half in range(2):
        pair = [part[:, half * across : (half + 1) * across] for part in parts]
        size = jnp.maximum(*(jnp.max(jnp.abs(part), -1, keepdims=True) for part in pair))
        shift = exponent(size)
        factor = jnp.exp2(-shift) * TOP
        extras = ((shift, high), (low, power))
        for which in range(2):
            for slot in range(16):
                if slot < lines:
                    line = jnp.floor(
                        pair[which][:, slot * LANES : (slot + 1) * LANES] * factor + 0.5
                    )
                    line = jnp.clip(line, -TOP, TOP)
                else:
                    line = jnp.broadcast_to(extras[which][slot - lines], (rows, LANES))
                wide[pl.ds(half * 32 + which * 16 + slot, rows, stride=64), :] = line
    out[...] = wide[...].astype(jnp.int32).astype(jnp.int16).reshape(out.shape)


def activate(got, out):
    coded = got[...].astype(jnp.int32).astype(F32)
    total = jnp.sum(coded * (jnp.exp2(coded[:, 14:15]) / TOP), 0)
    stats = (coded[:, 15:16] + coded[:, 30:31] / TOP) * (jnp.exp2(coded[:, 31:32]) / TOP)
    inv = lax.rsqrt(jnp.sum(stats, 0) / D + EPSILON)
    gate, up = total[:16] * inv, total[16:] * inv
    hidden = (gate * jax.nn.sigmoid(gate) * up).astype(BF16)
    out[...] = jnp.broadcast_to(hidden[None], out.shape)


def close(resid, got, out):
    total = resid[...] + jnp.sum(got[...], 0)
    out[...] = total.astype(BF16).reshape(out.shape)


def shards(
    tokens,
    norm_attn,
    norm_ffn,
    w_query,
    w_kv,
    w_out,
    w_gate_up,
    w_down,
    cache_keys,
    cache_values,
    lengths,
    owner,
):
    kv_count = lax.axis_size("kv")
    head_count = lax.axis_size("head")
    steps, rollouts, width = tokens.shape
    rows = steps * rollouts
    span, hd = cache_keys.shape[2:]
    shape = jax.ShapeDtypeStruct
    w_gate_up = w_gate_up.transpose(1, 0, 2)

    chunk = call(
        project,
        shape((kv_count * 8, hd), F32),
        (tokens, norm_attn, w_query, w_kv),
        [ANY] * 4,
        [pltpu.VMEM(x.shape, x.dtype) for x in (tokens, norm_attn, w_query, w_kv)]
        + [pltpu.VMEM((2 * width, hd), F32), pltpu.SemaphoreType.DMA((4,))],
        60,
    )
    got = exchange(chunk.reshape(kv_count, 8, hd), "kv", SCATTER)
    cache_shape = (rollouts, span, hd)
    keys, values = cache_keys.reshape(cache_shape), cache_values.reshape(cache_shape)
    mine = call(
        finish,
        shape((kv_count, 8, hd), BF16),
        (got, w_gate_up, values),
        [VMEM, ANY, VMEM],
        limit=51,
    )
    whole = exchange(mine, "kv", GATHER)

    chunk, stored = call(
        attend,
        (shape((kv_count, 8, hd), F32), shape((1, steps, rollouts, 1, 2, hd), BF16)),
        (lengths, owner, whole, keys, values),
        [VMEM] * 5,
    )
    got = exchange(chunk, "kv", SCATTER)
    context = exchange(call(combine, shape((kv_count, 4, hd), BF16), (got,)), "kv", GATHER)
    part = call(
        functools.partial(gathered_dot, 4),
        shape((head_count, rows, width), F32),
        (context, w_out),
        scratch=[pltpu.VMEM((kv_count * 4, hd), F32)],
    )
    got = exchange(part, "head", HEAD)

    resid, chunk = call(
        gate_up,
        (shape((rows, width), F32), shape((kv_count, 32, hd), jnp.int16)),
        (got, tokens, norm_ffn, w_gate_up),
        scratch=[pltpu.VMEM((kv_count * 32, hd), F32)],
    )
    got = exchange(chunk, "kv", SCATTER)
    hidden = exchange(call(activate, shape((kv_count, 16, hd), BF16), (got,)), "kv", GATHER)
    part = call(
        functools.partial(gathered_dot, w_down.shape[0] // 2 // hd),
        shape((head_count, rows, width), F32),
        (hidden, w_down),
        scratch=[pltpu.VMEM((kv_count * 16, hd), F32)],
    )
    got = exchange(part, "head", HEAD)
    layer_out = call(close, shape((steps, rollouts, width), BF16), (resid, got))
    return (layer_out, stored)


def solution(mesh):
    return jax.shard_map(
        shards,
        mesh=mesh,
        in_specs=(
            P(None, None, "kv"),
            P("kv"),
            P("kv"),
            P("kv", "head"),
            P("kv", None, "head"),
            P("head", "kv"),
            P("kv", None, "head"),
            P("head", "kv"),
            P(None, "head", "kv", None),
            P(None, "head", "kv", None),
            P(),
            P(),
        ),
        out_specs=(P(None, None, "kv"), P("kv", None, None, "head", None, None)),
        check_vma=False,
    )
```

```python
import functools

import jax
import jax.numpy as jnp
from jax import lax
from jax.experimental import pallas as pl
from jax.experimental.pallas import tpu as pltpu
from jax.sharding import PartitionSpec as P

D = 8192
EPSILON = 1e-05
NEGATIVE = -1e30
F32 = jnp.float32
BF16 = jnp.bfloat16
LANES = 128
TOP = 32767.0
VMEM = pl.BlockSpec(memory_space=pltpu.VMEM)
ANY = pl.BlockSpec(memory_space=pl.ANY)


def ring(sizes, first):
    major, minor = sizes
    return [
        (a + first[0]) % major * minor + (b + first[1]) % minor
        for a in range(major)
        for b in range(minor)
    ]


FIRST, KV = ring((8, 4), (5, 2)), ring((8, 4), (4, 2))
HEAD = [4, 5, 2, 6, 3, 7, 0, 1]
PLACE = [KV.index(device) for device in FIRST]


def exchange(x, axis, order):
    return lax.all_to_all(x, axis, 0, 0, tiled=True, axis_index_groups=[order])


def call(body, out_shape, args, specs=None, scratch=(), limit=24):
    return pl.pallas_call(
        body,
        out_shape=out_shape,
        in_specs=[VMEM] * len(args) if specs is None else specs,
        out_specs=jax.tree.map(lambda _: VMEM, out_shape),
        scratch_shapes=list(scratch),
        compiler_params=pltpu.CompilerParams(vmem_limit_bytes=int(limit * 2**20)),
    )(*args)


def project(
    tokens_at, gain_at, w_query_at, w_kv_at, out, tokens, gain, w_query, w_kv, wide, sems
):
    copies = [
        pltpu.make_async_copy(src, dst, sems.at[i])
        for i, (src, dst) in enumerate(
            ((w_kv_at, w_kv), (tokens_at, tokens), (gain_at, gain), (w_query_at, w_query))
        )
    ]
    for copy in copies:
        copy.start()
    for copy in copies[:3]:
        copy.wait()
    rows = tokens.shape[0] * tokens.shape[1]
    width = tokens.shape[2]
    wide[...] = w_kv[...].astype(F32).reshape(2 * width, LANES)
    flat = tokens[...].astype(F32).reshape(rows, tokens.shape[2])
    normed = (flat * gain[...].astype(F32).reshape(1, -1)).astype(BF16)
    kv = [
        jnp.dot(
            normed, wide[pl.ds(i, width, stride=2), :].astype(BF16), preferred_element_type=F32
        )
        for i in range(2)
    ]
    copies[3].wait()
    q = jnp.dot(normed, w_query[...], preferred_element_type=F32)
    stat = jnp.broadcast_to(jnp.sum(flat * flat, -1, keepdims=True), (rows, LANES))
    for half in range(2):
        for slot in range(8):
            if slot < 4:
                at = (half * 4 + slot) * LANES
                part = q[:, at : at + LANES]
            elif slot == 4:
                part = kv[half]
            else:
                part = stat
            out[pl.ds(half * 8 + slot, rows, stride=16), :] = part


def finish(got, relaid, values, out):
    total = jnp.sum(got[...], 0)
    inv = lax.rsqrt(total[7:8] / D + EPSILON)
    out[...] = jnp.broadcast_to((total * inv).astype(BF16)[None], out.shape)


def attend(lengths, owner, whole, keys, values, out, stored):
    rollouts, span, hd = keys.shape
    index = lax.axis_index("kv")
    live = lengths[...].reshape(1, rollouts) - index * span
    holder = owner[...].reshape(1, 2) == index
    scale = hd ** (-0.5)
    row = lax.broadcasted_iota(jnp.int32, (8, LANES), 0)
    lane = lax.broadcasted_iota(jnp.int32, (16, LANES), 1)
    column = lax.broadcasted_iota(jnp.int32, (16, span), 1)
    step = lax.broadcasted_iota(jnp.int32, (16, 1), 0) // 8
    here = index == 0
    queries, news = [], []
    for b in range(rollouts):
        tiles, pairs = [], []
        for s in range(2):
            at = (s * rollouts + b) * 2
            low = whole[PLACE[at]].astype(F32)
            high = whole[PLACE[at + 1]].astype(F32)
            tiles.append(jnp.where(row < 4, low, pltpu.roll(high, 4, 0)))
            pairs.append((low[4:5], high[4:5]))
            pair = jnp.concatenate(pairs[s], 0)
            mine = holder[:, s : s + 1]
            stored[0, s, b, 0] = jnp.where(mine, pair, jnp.zeros_like(pair)).astype(BF16)
        queries.append(jnp.concatenate(tiles, 0))
        news.append(pairs)
    scores = []
    for b in range(rollouts):
        scores.append(
            lax.dot_general(
                queries[b].astype(BF16),
                keys[b],
                (((1,), (1,)), ((), ())),
                preferred_element_type=F32,
            )
            * scale
        )
    weights, totals, tops, extras = [], [], [], []
    for b in range(rollouts):
        keep = column < live[:, b : b + 1]
        masked = jnp.where(keep, scores[b], NEGATIVE)
        top = jnp.max(masked, -1, keepdims=True)
        fresh = []
        for t in range(2):
            allowed = (step >= t) & here
            score = jnp.sum(queries[b] * news[b][t][0], -1, keepdims=True) * scale
            fresh.append((allowed, jnp.where(allowed, score, NEGATIVE)))
            top = jnp.maximum(top, fresh[t][1])
        e = jnp.where(keep, jnp.exp(masked - top), 0.0)
        extra = [jnp.where(ok, jnp.exp(score - top), 0.0) for ok, score in fresh]
        totals.append(jnp.sum(e, -1, keepdims=True) + extra[0] + extra[1])
        weights.append(e.astype(BF16))
        tops.append(top)
        extras.append(extra)
    for b in range(rollouts):
        sums = jnp.dot(weights[b], values[b], preferred_element_type=F32)
        for t in range(2):
            sums = sums + extras[b][t].astype(BF16).astype(F32) * news[b][t][1]
        stat = jnp.where(lane < LANES // 2, tops[b], totals[b])
        for s in range(2):
            sums_s, stat_s = sums[s * 8 : s * 8 + 8], stat[s * 8 : s * 8 + 8]
            at = (s * rollouts + b) * 2
            out[at] = jnp.where(row < 4, sums_s, pltpu.roll(stat_s, 4, 0))
            out[at + 1] = jnp.where(row < 4, pltpu.roll(sums_s, 4, 0), stat_s)


def combine(got, out):
    tops = got[:, 4:, :1]
    factor = jnp.exp(tops - jnp.max(tops, 0, keepdims=True))
    total = jnp.sum(factor * got[:, 4:, LANES // 2 : LANES // 2 + 1], 0)
    context = jnp.sum(factor * got[:, :4, :], 0) / total
    out[...] = jnp.broadcast_to(context.astype(BF16)[None], out.shape)


def gathered_dot(used, whole, w, out, wide):
    chunks, lines = whole.shape[:2]
    wide[...] = whole[...].astype(F32).reshape(chunks * lines, LANES)
    rows = chunks // 2
    parts = [
        wide[pl.ds(half * lines + slot, rows, stride=2 * lines), :].astype(BF16)
        for half in range(2)
        for slot in range(used)
    ]
    part = jnp.dot(jnp.concatenate(parts, 1), w[...], preferred_element_type=F32)
    out[...] = jnp.broadcast_to(part[None], out.shape)


def exponent(x):
    return jnp.ceil(jnp.log2(jnp.maximum(x, 1e-30)))


def gate_up(got, tokens, gain, w, resid_out, out, wide):
    rows, width = resid_out.shape
    resid = tokens[...].astype(F32).reshape(rows, width) + jnp.sum(got[...], 0)
    resid_out[...] = resid
    normed = (resid * gain[...].astype(F32).reshape(1, -1)).astype(BF16)
    stat = jnp.sum(resid * resid, -1, keepdims=True)
    power = exponent(stat)
    scaled = stat * jnp.exp2(-power) * TOP
    high = jnp.floor(scaled)
    low = jnp.floor((scaled - high) * TOP)
    lines = w.shape[2] // 2 // LANES
    across = lines * LANES
    parts = [jnp.dot(normed, w[which], preferred_element_type=F32) for which in range(2)]
    for half in range(2):
        pair = [part[:, half * across : (half + 1) * across] for part in parts]
        size = jnp.maximum(*(jnp.max(jnp.abs(part), -1, keepdims=True) for part in pair))
        shift = exponent(size)
        factor = jnp.exp2(-shift) * TOP
        extras = ((shift, high), (low, power))
        for which in range(2):
            for slot in range(16):
                if slot < lines:
                    line = jnp.floor(
                        pair[which][:, slot * LANES : (slot + 1) * LANES] * factor + 0.5
                    )
                    line = jnp.clip(line, -TOP, TOP)
                else:
                    line = jnp.broadcast_to(extras[which][slot - lines], (rows, LANES))
                wide[pl.ds(half * 32 + which * 16 + slot, rows, stride=64), :] = line
    out[...] = wide[...].astype(jnp.int32).astype(jnp.int16).reshape(out.shape)


def activate(got, out):
    coded = got[...].astype(jnp.int32).astype(F32)
    total = jnp.sum(coded * (jnp.exp2(coded[:, 14:15]) / TOP), 0)
    stats = (coded[:, 15:16] + coded[:, 30:31] / TOP) * (jnp.exp2(coded[:, 31:32]) / TOP)
    inv = lax.rsqrt(jnp.sum(stats, 0) / D + EPSILON)
    gate, up = total[:16] * inv, total[16:] * inv
    hidden = (gate * jax.nn.sigmoid(gate) * up).astype(BF16)
    out[...] = jnp.broadcast_to(hidden[None], out.shape)


def close(resid, got, out):
    total = resid[...] + jnp.sum(got[...], 0)
    out[...] = total.astype(BF16).reshape(out.shape)


def shards(
    tokens,
    norm_attn,
    norm_ffn,
    w_query,
    w_kv,
    w_out,
    w_gate_up,
    w_down,
    cache_keys,
    cache_values,
    lengths,
    owner,
):
    kv_count = lax.axis_size("kv")
    head_count = lax.axis_size("head")
    steps, rollouts, width = tokens.shape
    rows = steps * rollouts
    span, hd = cache_keys.shape[2:]
    shape = jax.ShapeDtypeStruct
    w_gate_up = w_gate_up.transpose(1, 0, 2)

    chunk = call(
        project,
        shape((kv_count * 8, hd), F32),
        (tokens, norm_attn, w_query, w_kv),
        [ANY] * 4,
        [pltpu.VMEM(x.shape, x.dtype) for x in (tokens, norm_attn, w_query, w_kv)]
        + [pltpu.VMEM((2 * width, hd), F32), pltpu.SemaphoreType.DMA((4,))],
        60,
    )
    got = exchange(chunk.reshape(kv_count, 8, hd), "kv", FIRST)
    cache_shape = (rollouts, span, hd)
    keys, values = cache_keys.reshape(cache_shape), cache_values.reshape(cache_shape)
    mine = call(
        finish,
        shape((kv_count, 8, hd), BF16),
        (got, w_gate_up, values),
        [VMEM, ANY, VMEM],
        limit=51,
    )
    whole = exchange(mine, "kv", KV)

    chunk, stored = call(
        attend,
        (shape((kv_count, 8, hd), F32), shape((1, steps, rollouts, 1, 2, hd), BF16)),
        (lengths, owner, whole, keys, values),
        [VMEM] * 5,
    )
    got = exchange(chunk, "kv", KV)
    context = exchange(call(combine, shape((kv_count, 4, hd), BF16), (got,)), "kv", KV)
    part = call(
        functools.partial(gathered_dot, 4),
        shape((head_count, rows, width), F32),
        (context, w_out),
        scratch=[pltpu.VMEM((kv_count * 4, hd), F32)],
    )
    got = exchange(part, "head", HEAD)

    resid, chunk = call(
        gate_up,
        (shape((rows, width), F32), shape((kv_count, 32, hd), jnp.int16)),
        (got, tokens, norm_ffn, w_gate_up),
        scratch=[pltpu.VMEM((kv_count * 32, hd), F32)],
    )
    got = exchange(chunk, "kv", KV)
    hidden = exchange(call(activate, shape((kv_count, 16, hd), BF16), (got,)), "kv", KV)
    part = call(
        functools.partial(gathered_dot, w_down.shape[0] // 2 // hd),
        shape((head_count, rows, width), F32),
        (hidden, w_down),
        scratch=[pltpu.VMEM((kv_count * 16, hd), F32)],
    )
    got = exchange(part, "head", HEAD)
    layer_out = call(close, shape((steps, rollouts, width), BF16), (resid, got))
    return (layer_out, stored)


def solution(mesh):
    return jax.shard_map(
        shards,
        mesh=mesh,
        in_specs=(
            P(None, None, "kv"),
            P("kv"),
            P("kv"),
            P("kv", "head"),
            P("kv", None, "head"),
            P("head", "kv"),
            P("kv", None, "head"),
            P("head", "kv"),
            P(None, "head", "kv", None),
            P(None, "head", "kv", None),
            P(),
            P(),
        ),
        out_specs=(P(None, None, "kv"), P("kv", None, None, "head", None, None)),
        check_vma=False,
    )
```

```python
import functools

import jax
import jax.numpy as jnp
from jax import lax
from jax.experimental import pallas as pl
from jax.experimental.pallas import tpu as pltpu
from jax.sharding import PartitionSpec as P

D = 8192
EPSILON = 1e-05
NEGATIVE = -1e30
F32 = jnp.float32
BF16 = jnp.bfloat16
LANES = 128
TOP = 32767.0
VMEM = pl.BlockSpec(memory_space=pltpu.VMEM)
ANY = pl.BlockSpec(memory_space=pl.ANY)


def ring(sizes, first):
    major, minor = sizes
    return [
        (a + first[0]) % major * minor + (b + first[1]) % minor
        for a in range(major)
        for b in range(minor)
    ]


FIRST, KV = ring((8, 4), (5, 2)), ring((8, 4), (4, 2))
HEAD, LAST = ring((4, 2), (2, 0)), [4, 5, 2, 6, 3, 7, 0, 1]
PLACE = [KV.index(device) for device in FIRST]


def exchange(x, axis, order):
    return lax.all_to_all(x, axis, 0, 0, tiled=True, axis_index_groups=[order])


def call(body, out_shape, args, specs=None, scratch=(), limit=24):
    return pl.pallas_call(
        body,
        out_shape=out_shape,
        in_specs=[VMEM] * len(args) if specs is None else specs,
        out_specs=jax.tree.map(lambda _: VMEM, out_shape),
        scratch_shapes=list(scratch),
        compiler_params=pltpu.CompilerParams(vmem_limit_bytes=int(limit * 2**20)),
    )(*args)


def project(
    tokens_at, gain_at, w_query_at, w_kv_at, out, tokens, gain, w_query, w_kv, wide, sems
):
    copies = [
        pltpu.make_async_copy(src, dst, sems.at[i])
        for i, (src, dst) in enumerate(
            ((w_kv_at, w_kv), (tokens_at, tokens), (gain_at, gain), (w_query_at, w_query))
        )
    ]
    for copy in copies:
        copy.start()
    for copy in copies[:3]:
        copy.wait()
    rows = tokens.shape[0] * tokens.shape[1]
    width = tokens.shape[2]
    wide[...] = w_kv[...].astype(F32).reshape(2 * width, LANES)
    flat = tokens[...].astype(F32).reshape(rows, tokens.shape[2])
    normed = (flat * gain[...].astype(F32).reshape(1, -1)).astype(BF16)
    kv = [
        jnp.dot(
            normed, wide[pl.ds(i, width, stride=2), :].astype(BF16), preferred_element_type=F32
        )
        for i in range(2)
    ]
    copies[3].wait()
    q = jnp.dot(normed, w_query[...], preferred_element_type=F32)
    stat = jnp.broadcast_to(jnp.sum(flat * flat, -1, keepdims=True), (rows, LANES))
    for half in range(2):
        for slot in range(8):
            if slot < 4:
                at = (half * 4 + slot) * LANES
                part = q[:, at : at + LANES]
            elif slot == 4:
                part = kv[half]
            else:
                part = stat
            out[pl.ds(half * 8 + slot, rows, stride=16), :] = part


def finish(got, relaid, values, out):
    total = jnp.sum(got[...], 0)
    inv = lax.rsqrt(total[7:8] / D + EPSILON)
    out[...] = jnp.broadcast_to((total * inv).astype(BF16)[None], out.shape)


def attend(lengths, owner, whole, keys, values, out, stored):
    rollouts, span, hd = keys.shape
    index = lax.axis_index("kv")
    live = lengths[...].reshape(1, rollouts) - index * span
    holder = owner[...].reshape(1, 2) == index
    scale = hd ** (-0.5)
    row = lax.broadcasted_iota(jnp.int32, (8, LANES), 0)
    lane = lax.broadcasted_iota(jnp.int32, (16, LANES), 1)
    column = lax.broadcasted_iota(jnp.int32, (16, span), 1)
    step = lax.broadcasted_iota(jnp.int32, (16, 1), 0) // 8
    here = index == 0
    queries, news = [], []
    for b in range(rollouts):
        tiles, pairs = [], []
        for s in range(2):
            at = (s * rollouts + b) * 2
            low = whole[PLACE[at]].astype(F32)
            high = whole[PLACE[at + 1]].astype(F32)
            tiles.append(jnp.where(row < 4, low, pltpu.roll(high, 4, 0)))
            pairs.append((low[4:5], high[4:5]))
            pair = jnp.concatenate(pairs[s], 0)
            mine = holder[:, s : s + 1]
            stored[0, s, b, 0] = jnp.where(mine, pair, jnp.zeros_like(pair)).astype(BF16)
        queries.append(jnp.concatenate(tiles, 0))
        news.append(pairs)
    scores = []
    for b in range(0, rollouts, 2):
        blank = jnp.zeros_like(queries[b])
        pair = jnp.concatenate(
            [
                jnp.concatenate([queries[b], blank], 1),
                jnp.concatenate([blank, queries[b + 1]], 1),
            ],
            0,
        )
        both = (
            lax.dot_general(
                pair.astype(BF16),
                jnp.concatenate([keys[b], keys[b + 1]], 1),
                (((1,), (1,)), ((), ())),
                preferred_element_type=F32,
            )
            * scale
        )
        scores += [both[:16], both[16:]]
    weights, totals, tops, extras = [], [], [], []
    for b in range(rollouts):
        keep = column < live[:, b : b + 1]
        masked = jnp.where(keep, scores[b], NEGATIVE)
        top = jnp.max(masked, -1, keepdims=True)
        fresh = []
        for t in range(2):
            allowed = (step >= t) & here
            score = jnp.sum(queries[b] * news[b][t][0], -1, keepdims=True) * scale
            fresh.append((allowed, jnp.where(allowed, score, NEGATIVE)))
            top = jnp.maximum(top, fresh[t][1])
        e = jnp.where(keep, jnp.exp(masked - top), 0.0)
        extra = [jnp.where(ok, jnp.exp(score - top), 0.0) for ok, score in fresh]
        totals.append(jnp.sum(e, -1, keepdims=True) + extra[0] + extra[1])
        weights.append(e.astype(BF16))
        tops.append(top)
        extras.append(extra)
    weighted = []
    for b in range(0, rollouts, 2):
        both = jnp.dot(
            jnp.concatenate([weights[b], weights[b + 1]], 0),
            jnp.concatenate([values[b], values[b + 1]], 1),
            preferred_element_type=F32,
        )
        weighted += [both[:16, :hd], both[16:, hd:]]
    for b in range(rollouts):
        sums = weighted[b]
        for t in range(2):
            sums = sums + extras[b][t].astype(BF16).astype(F32) * news[b][t][1]
        stat = jnp.where(lane < LANES // 2, tops[b], totals[b])
        for s in range(2):
            sums_s, stat_s = sums[s * 8 : s * 8 + 8], stat[s * 8 : s * 8 + 8]
            at = (s * rollouts + b) * 2
            out[at] = jnp.where(row < 4, sums_s, pltpu.roll(stat_s, 4, 0))
            out[at + 1] = jnp.where(row < 4, pltpu.roll(sums_s, 4, 0), stat_s)


def combine(got, out):
    tops = got[:, 4:, :1]
    factor = jnp.exp(tops - jnp.max(tops, 0, keepdims=True))
    total = jnp.sum(factor * got[:, 4:, LANES // 2 : LANES // 2 + 1], 0)
    context = jnp.sum(factor * got[:, :4, :], 0) / total
    out[...] = jnp.broadcast_to(context.astype(BF16)[None], out.shape)


def gathered_dot(used, whole, w, out, wide):
    chunks, lines = whole.shape[:2]
    wide[...] = whole[...].astype(F32).reshape(chunks * lines, LANES)
    rows = chunks // 2
    parts = [
        wide[pl.ds(half * lines + slot, rows, stride=2 * lines), :].astype(BF16)
        for half in range(2)
        for slot in range(used)
    ]
    part = jnp.dot(jnp.concatenate(parts, 1), w[...], preferred_element_type=F32)
    out[...] = jnp.broadcast_to(part[None], out.shape)


def exponent(x):
    return jnp.ceil(jnp.log2(jnp.maximum(x, 1e-30)))


def gate_up(got, tokens, gain, w, resid_out, out, wide):
    rows, width = resid_out.shape
    resid = tokens[...].astype(F32).reshape(rows, width) + jnp.sum(got[...], 0)
    resid_out[...] = resid
    normed = (resid * gain[...].astype(F32).reshape(1, -1)).astype(BF16)
    stat = jnp.sum(resid * resid, -1, keepdims=True)
    power = exponent(stat)
    scaled = stat * jnp.exp2(-power) * TOP
    high = jnp.floor(scaled)
    low = jnp.floor((scaled - high) * TOP)
    lines = w.shape[2] // 2 // LANES
    across = lines * LANES
    parts = [jnp.dot(normed, w[which], preferred_element_type=F32) for which in range(2)]
    for half in range(2):
        pair = [part[:, half * across : (half + 1) * across] for part in parts]
        size = jnp.maximum(*(jnp.max(jnp.abs(part), -1, keepdims=True) for part in pair))
        shift = exponent(size)
        factor = jnp.exp2(-shift) * TOP
        extras = ((shift, high), (low, power))
        for which in range(2):
            for slot in range(16):
                if slot < lines:
                    line = jnp.floor(
                        pair[which][:, slot * LANES : (slot + 1) * LANES] * factor + 0.5
                    )
                    line = jnp.clip(line, -TOP, TOP)
                else:
                    line = jnp.broadcast_to(extras[which][slot - lines], (rows, LANES))
                wide[pl.ds(half * 32 + which * 16 + slot, rows, stride=64), :] = line
    out[...] = wide[...].astype(jnp.int32).astype(jnp.int16).reshape(out.shape)


def activate(got, out):
    coded = got[...].astype(jnp.int32).astype(F32)
    total = jnp.sum(coded * (jnp.exp2(coded[:, 14:15]) / TOP), 0)
    stats = (coded[:, 15:16] + coded[:, 30:31] / TOP) * (jnp.exp2(coded[:, 31:32]) / TOP)
    inv = lax.rsqrt(jnp.sum(stats, 0) / D + EPSILON)
    gate, up = total[:16] * inv, total[16:] * inv
    hidden = (gate * jax.nn.sigmoid(gate) * up).astype(BF16)
    out[...] = jnp.broadcast_to(hidden[None], out.shape)


def close(resid, got, out):
    total = resid[...] + jnp.sum(got[...], 0)
    out[...] = total.astype(BF16).reshape(out.shape)


def shards(
    tokens,
    norm_attn,
    norm_ffn,
    w_query,
    w_kv,
    w_out,
    w_gate_up,
    w_down,
    cache_keys,
    cache_values,
    lengths,
    owner,
):
    kv_count = lax.axis_size("kv")
    head_count = lax.axis_size("head")
    steps, rollouts, width = tokens.shape
    rows = steps * rollouts
    span, hd = cache_keys.shape[2:]
    shape = jax.ShapeDtypeStruct
    w_gate_up = w_gate_up.transpose(1, 0, 2)

    chunk = call(
        project,
        shape((kv_count * 8, hd), F32),
        (tokens, norm_attn, w_query, w_kv),
        [ANY] * 4,
        [pltpu.VMEM(x.shape, x.dtype) for x in (tokens, norm_attn, w_query, w_kv)]
        + [pltpu.VMEM((2 * width, hd), F32), pltpu.SemaphoreType.DMA((4,))],
        60,
    )
    got = exchange(chunk.reshape(kv_count, 8, hd), "kv", FIRST)
    cache_shape = (rollouts, span, hd)
    keys, values = cache_keys.reshape(cache_shape), cache_values.reshape(cache_shape)
    mine = call(
        finish,
        shape((kv_count, 8, hd), BF16),
        (got, w_gate_up, values),
        [VMEM, ANY, VMEM],
        limit=51,
    )
    whole = exchange(mine, "kv", KV)

    chunk, stored = call(
        attend,
        (shape((kv_count, 8, hd), F32), shape((1, steps, rollouts, 1, 2, hd), BF16)),
        (lengths, owner, whole, keys, values),
        [VMEM] * 5,
    )
    got = exchange(chunk, "kv", KV)
    context = exchange(call(combine, shape((kv_count, 4, hd), BF16), (got,)), "kv", KV)
    part = call(
        functools.partial(gathered_dot, 4),
        shape((head_count, rows, width), F32),
        (context, w_out),
        scratch=[pltpu.VMEM((kv_count * 4, hd), F32)],
    )
    got = exchange(part, "head", HEAD)

    resid, chunk = call(
        gate_up,
        (shape((rows, width), F32), shape((kv_count, 32, hd), jnp.int16)),
        (got, tokens, norm_ffn, w_gate_up),
        scratch=[pltpu.VMEM((kv_count * 32, hd), F32)],
    )
    got = exchange(chunk, "kv", KV)
    hidden = exchange(call(activate, shape((kv_count, 16, hd), BF16), (got,)), "kv", KV)
    part = call(
        functools.partial(gathered_dot, w_down.shape[0] // 2 // hd),
        shape((head_count, rows, width), F32),
        (hidden, w_down),
        scratch=[pltpu.VMEM((kv_count * 16, hd), F32)],
    )
    got = exchange(part, "head", LAST)
    layer_out = call(close, shape((steps, rollouts, width), BF16), (resid, got))
    return (layer_out, stored)


def solution(mesh):
    return jax.shard_map(
        shards,
        mesh=mesh,
        in_specs=(
            P(None, None, "kv"),
            P("kv"),
            P("kv"),
            P("kv", "head"),
            P("kv", None, "head"),
            P("head", "kv"),
            P("kv", None, "head"),
            P("head", "kv"),
            P(None, "head", "kv", None),
            P(None, "head", "kv", None),
            P(),
            P(),
        ),
        out_specs=(P(None, None, "kv"), P("kv", None, None, "head", None, None)),
        check_vma=False,
    )
```

```python
import functools

import jax
import jax.numpy as jnp
from jax import lax
from jax.experimental import pallas as pl
from jax.experimental.pallas import tpu as pltpu
from jax.sharding import PartitionSpec as P

D = 8192
EPSILON = 1e-05
NEGATIVE = -1e30
F32 = jnp.float32
BF16 = jnp.bfloat16
LANES = 128
TOP = 32700.0
VMEM = pl.BlockSpec(memory_space=pltpu.VMEM)
ANY = pl.BlockSpec(memory_space=pl.ANY)


def ring(sizes, first):
    major, minor = sizes
    return [
        (a + first[0]) % major * minor + (b + first[1]) % minor
        for a in range(major)
        for b in range(minor)
    ]


FIRST, KV = ring((8, 4), (5, 2)), ring((8, 4), (4, 2))
HEAD, LAST = ring((4, 2), (2, 0)), [4, 5, 2, 6, 3, 7, 0, 1]
PLACE = [KV.index(device) for device in FIRST]


def exchange(x, axis, order):
    return lax.all_to_all(x, axis, 0, 0, tiled=True, axis_index_groups=[order])


def call(body, out_shape, args, specs=None, scratch=(), limit=24):
    return pl.pallas_call(
        body,
        out_shape=out_shape,
        in_specs=[VMEM] * len(args) if specs is None else specs,
        out_specs=jax.tree.map(lambda _: VMEM, out_shape),
        scratch_shapes=list(scratch),
        compiler_params=pltpu.CompilerParams(vmem_limit_bytes=int(limit * 2**20)),
    )(*args)


def project(
    tokens_at, gain_at, w_query_at, w_kv_at, out, tokens, gain, w_query, w_kv, wide, sems
):
    across = w_query.shape[1] // 2
    sides = [pl.ds(half * across, across) for half in range(2)]
    pairs = [(w_kv_at, w_kv), (tokens_at, tokens), (gain_at, gain)]
    pairs += [(w_query_at.at[:, side], w_query.at[:, side]) for side in sides]
    copies = [
        pltpu.make_async_copy(src, dst, sems.at[i]) for i, (src, dst) in enumerate(pairs)
    ]
    for copy in copies:
        copy.start()
    for copy in copies[:3]:
        copy.wait()
    rows = tokens.shape[0] * tokens.shape[1]
    width = tokens.shape[2]
    wide[...] = w_kv[...].astype(F32).reshape(2 * width, LANES)
    flat = tokens[...].astype(F32).reshape(rows, tokens.shape[2])
    normed = (flat * gain[...].astype(F32).reshape(1, -1)).astype(BF16)
    kv = [
        jnp.dot(
            normed, wide[pl.ds(i, width, stride=2), :].astype(BF16), preferred_element_type=F32
        )
        for i in range(2)
    ]
    stat = jnp.broadcast_to(jnp.sum(flat * flat, -1, keepdims=True), (rows, LANES))
    for half in range(2):
        copies[3 + half].wait()
        q = jnp.dot(normed, w_query[:, sides[half]], preferred_element_type=F32)
        for slot in range(8):
            if slot < 4:
                part = q[:, slot * LANES : (slot + 1) * LANES]
            elif slot == 4:
                part = kv[half]
            else:
                part = stat
            out[pl.ds(half * 8 + slot, rows, stride=16), :] = part


def finish(got, relaid, values, out):
    total = jnp.sum(got[...], 0)
    inv = lax.rsqrt(total[7:8] / D + EPSILON)
    out[...] = jnp.broadcast_to((total * inv).astype(BF16)[None], out.shape)


def attend(lengths, owner, whole, keys, values, out, stored):
    rollouts, span, hd = keys.shape
    index = lax.axis_index("kv")
    live = lengths[...].reshape(1, rollouts) - index * span
    holder = owner[...].reshape(1, 2) == index
    scale = hd ** (-0.5)
    row = lax.broadcasted_iota(jnp.int32, (8, LANES), 0)
    lane = lax.broadcasted_iota(jnp.int32, (16, LANES), 1)
    column = lax.broadcasted_iota(jnp.int32, (16, span), 1)
    step = lax.broadcasted_iota(jnp.int32, (16, 1), 0) // 8
    here = index == 0
    queries, news = [], []
    for b in range(rollouts):
        tiles, pairs = [], []
        for s in range(2):
            at = (s * rollouts + b) * 2
            low = whole[PLACE[at]].astype(F32)
            high = whole[PLACE[at + 1]].astype(F32)
            tiles.append(jnp.where(row < 4, low, pltpu.roll(high, 4, 0)))
            pairs.append((low[4:5], high[4:5]))
            pair = jnp.concatenate(pairs[s], 0)
            mine = holder[:, s : s + 1]
            stored[0, s, b, 0] = jnp.where(mine, pair, jnp.zeros_like(pair)).astype(BF16)
        queries.append(jnp.concatenate(tiles, 0))
        news.append(pairs)
    scores = []
    for b in range(rollouts):
        scores.append(
            lax.dot_general(
                queries[b].astype(BF16),
                keys[b],
                (((1,), (1,)), ((), ())),
                preferred_element_type=F32,
            )
            * scale
        )
    weights, totals, tops, extras = [], [], [], []
    for b in range(rollouts):
        keep = column < live[:, b : b + 1]
        masked = jnp.where(keep, scores[b], NEGATIVE)
        top = jnp.max(masked, -1, keepdims=True)
        fresh = []
        for t in range(2):
            allowed = (step >= t) & here
            score = jnp.sum(queries[b] * news[b][t][0], -1, keepdims=True) * scale
            fresh.append((allowed, jnp.where(allowed, score, NEGATIVE)))
            top = jnp.maximum(top, fresh[t][1])
        e = jnp.where(keep, jnp.exp(masked - top), 0.0)
        extra = [jnp.where(ok, jnp.exp(score - top), 0.0) for ok, score in fresh]
        totals.append(jnp.sum(e, -1, keepdims=True) + extra[0] + extra[1])
        weights.append(e.astype(BF16))
        tops.append(top)
        extras.append(extra)
    for b in range(rollouts):
        sums = jnp.dot(weights[b], values[b], preferred_element_type=F32)
        for t in range(2):
            sums = sums + extras[b][t].astype(BF16).astype(F32) * news[b][t][1]
        stat = jnp.where(lane < LANES // 2, tops[b], totals[b])
        for s in range(2):
            sums_s, stat_s = sums[s * 8 : s * 8 + 8], stat[s * 8 : s * 8 + 8]
            at = (s * rollouts + b) * 2
            out[at] = jnp.where(row < 4, sums_s, pltpu.roll(stat_s, 4, 0))
            out[at + 1] = jnp.where(row < 4, pltpu.roll(sums_s, 4, 0), stat_s)


def combine(got, out):
    tops = got[:, 4:, :1]
    factor = jnp.exp(tops - jnp.max(tops, 0, keepdims=True))
    total = jnp.sum(factor * got[:, 4:, LANES // 2 : LANES // 2 + 1], 0)
    context = jnp.sum(factor * got[:, :4, :], 0) / total
    out[...] = jnp.broadcast_to(context.astype(BF16)[None], out.shape)


def gathered_dot(used, whole, w, out, wide):
    chunks, lines = whole.shape[:2]
    wide[...] = whole[...].astype(F32).reshape(chunks * lines, LANES)
    rows = chunks // 2
    parts = [
        wide[pl.ds(half * lines + slot, rows, stride=2 * lines), :].astype(BF16)
        for half in range(2)
        for slot in range(used)
    ]
    part = jnp.dot(jnp.concatenate(parts, 1), w[...], preferred_element_type=F32)
    out[...] = jnp.broadcast_to(part[None], out.shape)


def exponent(x):
    return jnp.ceil(jnp.log2(jnp.maximum(x, 1e-30)))


def gate_up(got, tokens, gain, w, resid_out, out, wide):
    rows, width = resid_out.shape
    resid = tokens[...].astype(F32).reshape(rows, width) + jnp.sum(got[...], 0)
    resid_out[...] = resid
    normed = (resid * gain[...].astype(F32).reshape(1, -1)).astype(BF16)
    stat = jnp.sum(resid * resid, -1, keepdims=True)
    power = exponent(stat)
    scaled = stat * jnp.exp2(-power) * TOP
    high = jnp.floor(scaled)
    low = jnp.floor((scaled - high) * TOP)
    lines = w.shape[2] // 2 // LANES
    across = lines * LANES
    parts = [jnp.dot(normed, w[which], preferred_element_type=F32) for which in range(2)]
    for half in range(2):
        pair = [part[:, half * across : (half + 1) * across] for part in parts]
        size = jnp.maximum(*(jnp.max(jnp.abs(part), -1, keepdims=True) for part in pair))
        shift = exponent(size)
        factor = jnp.exp2(-shift) * TOP
        extras = ((shift, high), (low, power))
        for which in range(2):
            for slot in range(16):
                if slot < lines:
                    line = jnp.floor(
                        pair[which][:, slot * LANES : (slot + 1) * LANES] * factor + 0.5
                    )
                else:
                    line = jnp.broadcast_to(extras[which][slot - lines], (rows, LANES))
                wide[pl.ds(half * 32 + which * 16 + slot, rows, stride=64), :] = line
    out[...] = wide[...].astype(jnp.int32).astype(jnp.int16).reshape(out.shape)


def activate(got, out):
    coded = got[...].astype(jnp.int32).astype(F32)
    total = jnp.sum(coded * (jnp.exp2(coded[:, 14:15]) / TOP), 0)
    stats = (coded[:, 15:16] + coded[:, 30:31] / TOP) * (jnp.exp2(coded[:, 31:32]) / TOP)
    inv = lax.rsqrt(jnp.sum(stats, 0) / D + EPSILON)
    gate, up = total[:16] * inv, total[16:] * inv
    hidden = (gate * jax.nn.sigmoid(gate) * up).astype(BF16)
    out[...] = jnp.broadcast_to(hidden[None], out.shape)


def close(resid, got, out):
    total = resid[...] + jnp.sum(got[...], 0)
    out[...] = total.astype(BF16).reshape(out.shape)


def shards(
    tokens,
    norm_attn,
    norm_ffn,
    w_query,
    w_kv,
    w_out,
    w_gate_up,
    w_down,
    cache_keys,
    cache_values,
    lengths,
    owner,
):
    kv_count = lax.axis_size("kv")
    head_count = lax.axis_size("head")
    steps, rollouts, width = tokens.shape
    rows = steps * rollouts
    span, hd = cache_keys.shape[2:]
    shape = jax.ShapeDtypeStruct
    w_gate_up = w_gate_up.transpose(1, 0, 2)

    chunk = call(
        project,
        shape((kv_count * 8, hd), F32),
        (tokens, norm_attn, w_query, w_kv),
        [ANY] * 4,
        [pltpu.VMEM(x.shape, x.dtype) for x in (tokens, norm_attn, w_query, w_kv)]
        + [pltpu.VMEM((2 * width, hd), F32), pltpu.SemaphoreType.DMA((5,))],
        60,
    )
    got = exchange(chunk.reshape(kv_count, 8, hd), "kv", FIRST)
    cache_shape = (rollouts, span, hd)
    keys, values = cache_keys.reshape(cache_shape), cache_values.reshape(cache_shape)
    mine = call(
        finish,
        shape((kv_count, 8, hd), BF16),
        (got, w_gate_up, values),
        [VMEM, ANY, VMEM],
        limit=51,
    )
    whole = exchange(mine, "kv", KV)

    chunk, stored = call(
        attend,
        (shape((kv_count, 8, hd), F32), shape((1, steps, rollouts, 1, 2, hd), BF16)),
        (lengths, owner, whole, keys, values),
        [VMEM] * 5,
    )
    got = exchange(chunk, "kv", KV)
    context = exchange(call(combine, shape((kv_count, 4, hd), BF16), (got,)), "kv", KV)
    part = call(
        functools.partial(gathered_dot, 4),
        shape((head_count, rows, width), F32),
        (context, w_out),
        scratch=[pltpu.VMEM((kv_count * 4, hd), F32)],
    )
    got = exchange(part, "head", HEAD)

    resid, chunk = call(
        gate_up,
        (shape((rows, width), F32), shape((kv_count, 32, hd), jnp.int16)),
        (got, tokens, norm_ffn, w_gate_up),
        scratch=[pltpu.VMEM((kv_count * 32, hd), F32)],
    )
    got = exchange(chunk, "kv", KV)
    hidden = exchange(call(activate, shape((kv_count, 16, hd), BF16), (got,)), "kv", KV)
    part = call(
        functools.partial(gathered_dot, w_down.shape[0] // 2 // hd),
        shape((head_count, rows, width), F32),
        (hidden, w_down),
        scratch=[pltpu.VMEM((kv_count * 16, hd), F32)],
    )
    got = exchange(part, "head", LAST)
    layer_out = call(close, shape((steps, rollouts, width), BF16), (resid, got))
    return (layer_out, stored)


def solution(mesh):
    return jax.shard_map(
        shards,
        mesh=mesh,
        in_specs=(
            P(None, None, "kv"),
            P("kv"),
            P("kv"),
            P("kv", "head"),
            P("kv", None, "head"),
            P("head", "kv"),
            P("kv", None, "head"),
            P("head", "kv"),
            P(None, "head", "kv", None),
            P(None, "head", "kv", None),
            P(),
            P(),
        ),
        out_specs=(P(None, None, "kv"), P("kv", None, None, "head", None, None)),
        check_vma=False,
    )
```

```python
import functools

import jax
import jax.numpy as jnp
from jax import lax
from jax.experimental import pallas as pl
from jax.experimental.pallas import tpu as pltpu
from jax.sharding import PartitionSpec as P

D = 8192
EPSILON = 1e-05
NEGATIVE = -1e30
F32 = jnp.float32
BF16 = jnp.bfloat16
LANES = 128
TOP = 32767.0
VMEM = pl.BlockSpec(memory_space=pltpu.VMEM)
ANY = pl.BlockSpec(memory_space=pl.ANY)


def ring(sizes, first):
    major, minor = sizes
    return [
        (a + first[0]) % major * minor + (b + first[1]) % minor
        for b in range(minor)
        for a in range(major)
    ]


ORDER = {"kv": ring((8, 4), (4, 2)), "head": [4, 5, 6, 7, 0, 1, 2, 3]}


def exchange(x, axis):
    return lax.all_to_all(x, axis, 0, 0, tiled=True, axis_index_groups=[ORDER[axis]])


def call(body, out_shape, args, specs=None, scratch=(), limit=24):
    return pl.pallas_call(
        body,
        out_shape=out_shape,
        in_specs=[VMEM] * len(args) if specs is None else specs,
        out_specs=jax.tree.map(lambda _: VMEM, out_shape),
        scratch_shapes=list(scratch),
        compiler_params=pltpu.CompilerParams(vmem_limit_bytes=int(limit * 2**20)),
    )(*args)


def project(
    tokens_at, gain_at, w_query_at, w_kv_at, out, tokens, gain, w_query, w_kv, wide, sems
):
    copies = [
        pltpu.make_async_copy(src, dst, sems.at[i])
        for i, (src, dst) in enumerate(
            ((w_kv_at, w_kv), (tokens_at, tokens), (gain_at, gain), (w_query_at, w_query))
        )
    ]
    for copy in copies:
        copy.start()
    for copy in copies[:3]:
        copy.wait()
    rows = tokens.shape[0] * tokens.shape[1]
    width = tokens.shape[2]
    wide[...] = w_kv[...].astype(F32).reshape(2 * width, LANES)
    flat = tokens[...].astype(F32).reshape(rows, tokens.shape[2])
    normed = (flat * gain[...].astype(F32).reshape(1, -1)).astype(BF16)
    kv = [
        jnp.dot(
            normed, wide[pl.ds(i, width, stride=2), :].astype(BF16), preferred_element_type=F32
        )
        for i in range(2)
    ]
    copies[3].wait()
    q = jnp.dot(normed, w_query[...], preferred_element_type=F32)
    stat = jnp.broadcast_to(jnp.sum(flat * flat, -1, keepdims=True), (rows, LANES))
    for half in range(2):
        for slot in range(8):
            if slot < 4:
                at = (half * 4 + slot) * LANES
                part = q[:, at : at + LANES]
            elif slot == 4:
                part = kv[half]
            else:
                part = stat
            out[pl.ds(half * 8 + slot, rows, stride=16), :] = part


def finish(got, relaid, values, out):
    total = jnp.sum(got[...], 0)
    inv = lax.rsqrt(total[7:8] / D + EPSILON)
    out[...] = jnp.broadcast_to((total * inv).astype(BF16)[None], out.shape)


def attend(lengths, owner, whole, keys, values, out, stored):
    rollouts, span, hd = keys.shape
    index = lax.axis_index("kv")
    live = lengths[...].reshape(1, rollouts) - index * span
    holder = owner[...].reshape(1, 2) == index
    scale = hd ** (-0.5)
    row = lax.broadcasted_iota(jnp.int32, (8, LANES), 0)
    lane = lax.broadcasted_iota(jnp.int32, (16, LANES), 1)
    column = lax.broadcasted_iota(jnp.int32, (16, span), 1)
    step = lax.broadcasted_iota(jnp.int32, (16, 1), 0) // 8
    here = index == 0
    queries, news = [], []
    for b in range(rollouts):
        tiles, pairs = [], []
        for s in range(2):
            low = whole[(s * rollouts + b) * 2].astype(F32)
            high = whole[(s * rollouts + b) * 2 + 1].astype(F32)
            tiles.append(jnp.where(row < 4, low, pltpu.roll(high, 4, 0)))
            pairs.append((low[4:5], high[4:5]))
            pair = jnp.concatenate(pairs[s], 0)
            mine = holder[:, s : s + 1]
            stored[0, s, b, 0] = jnp.where(mine, pair, jnp.zeros_like(pair)).astype(BF16)
        queries.append(jnp.concatenate(tiles, 0))
        news.append(pairs)
    scores = []
    for b in range(rollouts):
        scores.append(
            lax.dot_general(
                queries[b].astype(BF16),
                keys[b],
                (((1,), (1,)), ((), ())),
                preferred_element_type=F32,
            )
            * scale
        )
    weights, totals, tops, extras = [], [], [], []
    for b in range(rollouts):
        keep = column < live[:, b : b + 1]
        masked = jnp.where(keep, scores[b], NEGATIVE)
        top = jnp.max(masked, -1, keepdims=True)
        fresh = []
        for t in range(2):
            allowed = (step >= t) & here
            score = jnp.sum(queries[b] * news[b][t][0], -1, keepdims=True) * scale
            fresh.append((allowed, jnp.where(allowed, score, NEGATIVE)))
            top = jnp.maximum(top, fresh[t][1])
        e = jnp.where(keep, jnp.exp(masked - top), 0.0)
        extra = [jnp.where(ok, jnp.exp(score - top), 0.0) for ok, score in fresh]
        totals.append(jnp.sum(e, -1, keepdims=True) + extra[0] + extra[1])
        weights.append(e.astype(BF16))
        tops.append(top)
        extras.append(extra)
    for b in range(rollouts):
        sums = jnp.dot(weights[b], values[b], preferred_element_type=F32)
        for t in range(2):
            sums = sums + extras[b][t].astype(BF16).astype(F32) * news[b][t][1]
        stat = jnp.where(lane < LANES // 2, tops[b], totals[b])
        for s in range(2):
            sums_s, stat_s = sums[s * 8 : s * 8 + 8], stat[s * 8 : s * 8 + 8]
            at = (s * rollouts + b) * 2
            out[at] = jnp.where(row < 4, sums_s, pltpu.roll(stat_s, 4, 0))
            out[at + 1] = jnp.where(row < 4, pltpu.roll(sums_s, 4, 0), stat_s)


def combine(got, out):
    tops = got[:, 4:, :1]
    factor = jnp.exp(tops - jnp.max(tops, 0, keepdims=True))
    total = jnp.sum(factor * got[:, 4:, LANES // 2 : LANES // 2 + 1], 0)
    context = jnp.sum(factor * got[:, :4, :], 0) / total
    out[...] = jnp.broadcast_to(context.astype(BF16)[None], out.shape)


def gathered_dot(used, whole, w, out, wide):
    chunks, lines = whole.shape[:2]
    wide[...] = whole[...].astype(F32).reshape(chunks * lines, LANES)
    rows = chunks // 2
    parts = [
        wide[pl.ds(half * lines + slot, rows, stride=2 * lines), :].astype(BF16)
        for half in range(2)
        for slot in range(used)
    ]
    part = jnp.dot(jnp.concatenate(parts, 1), w[...], preferred_element_type=F32)
    out[...] = jnp.broadcast_to(part[None], out.shape)


def exponent(x):
    return jnp.ceil(jnp.log2(jnp.maximum(x, 1e-30)))


def gate_up(got, tokens, gain, w, resid_out, out, wide):
    rows, width = resid_out.shape
    resid = tokens[...].astype(F32).reshape(rows, width) + jnp.sum(got[...], 0)
    resid_out[...] = resid
    normed = (resid * gain[...].astype(F32).reshape(1, -1)).astype(BF16)
    stat = jnp.sum(resid * resid, -1, keepdims=True)
    power = exponent(stat)
    scaled = stat * jnp.exp2(-power) * TOP
    high = jnp.floor(scaled)
    low = jnp.floor((scaled - high) * TOP)
    lines = w.shape[2] // 2 // LANES
    across = lines * LANES
    parts = [jnp.dot(normed, w[which], preferred_element_type=F32) for which in range(2)]
    for half in range(2):
        pair = [part[:, half * across : (half + 1) * across] for part in parts]
        size = jnp.maximum(*(jnp.max(jnp.abs(part), -1, keepdims=True) for part in pair))
        shift = exponent(size)
        factor = jnp.exp2(-shift) * TOP
        extras = ((shift, high), (low, power))
        for which in range(2):
            for slot in range(16):
                if slot < lines:
                    line = jnp.floor(
                        pair[which][:, slot * LANES : (slot + 1) * LANES] * factor + 0.5
                    )
                    line = jnp.clip(line, -TOP, TOP)
                else:
                    line = jnp.broadcast_to(extras[which][slot - lines], (rows, LANES))
                wide[pl.ds(half * 32 + which * 16 + slot, rows, stride=64), :] = line
    out[...] = wide[...].astype(jnp.int32).astype(jnp.int16).reshape(out.shape)


def activate(got, out):
    coded = got[...].astype(jnp.int32).astype(F32)
    total = jnp.sum(coded * (jnp.exp2(coded[:, 14:15]) / TOP), 0)
    stats = (coded[:, 15:16] + coded[:, 30:31] / TOP) * (jnp.exp2(coded[:, 31:32]) / TOP)
    inv = lax.rsqrt(jnp.sum(stats, 0) / D + EPSILON)
    gate, up = total[:16] * inv, total[16:] * inv
    hidden = (gate * jax.nn.sigmoid(gate) * up).astype(BF16)
    out[...] = jnp.broadcast_to(hidden[None], out.shape)


def close(resid, got, out):
    total = resid[...] + jnp.sum(got[...], 0)
    out[...] = total.astype(BF16).reshape(out.shape)


def shards(
    tokens,
    norm_attn,
    norm_ffn,
    w_query,
    w_kv,
    w_out,
    w_gate_up,
    w_down,
    cache_keys,
    cache_values,
    lengths,
    owner,
):
    kv_count = lax.axis_size("kv")
    head_count = lax.axis_size("head")
    steps, rollouts, width = tokens.shape
    rows = steps * rollouts
    span, hd = cache_keys.shape[2:]
    shape = jax.ShapeDtypeStruct
    w_gate_up = w_gate_up.transpose(1, 0, 2)

    chunk = call(
        project,
        shape((kv_count * 8, hd), F32),
        (tokens, norm_attn, w_query, w_kv),
        [ANY] * 4,
        [pltpu.VMEM(x.shape, x.dtype) for x in (tokens, norm_attn, w_query, w_kv)]
        + [pltpu.VMEM((2 * width, hd), F32), pltpu.SemaphoreType.DMA((4,))],
        60,
    )
    got = exchange(chunk.reshape(kv_count, 8, hd), "kv")
    cache_shape = (rollouts, span, hd)
    keys, values = cache_keys.reshape(cache_shape), cache_values.reshape(cache_shape)
    mine = call(
        finish,
        shape((kv_count, 8, hd), BF16),
        (got, w_gate_up, values),
        [VMEM, ANY, VMEM],
        limit=51,
    )
    whole = exchange(mine, "kv")

    chunk, stored = call(
        attend,
        (shape((kv_count, 8, hd), F32), shape((1, steps, rollouts, 1, 2, hd), BF16)),
        (lengths, owner, whole, keys, values),
        [VMEM] * 5,
    )
    got = exchange(chunk, "kv")
    context = exchange(call(combine, shape((kv_count, 4, hd), BF16), (got,)), "kv")
    part = call(
        functools.partial(gathered_dot, 4),
        shape((head_count, rows, width), F32),
        (context, w_out),
        scratch=[pltpu.VMEM((kv_count * 4, hd), F32)],
    )
    got = exchange(part, "head")

    resid, chunk = call(
        gate_up,
        (shape((rows, width), F32), shape((kv_count, 32, hd), jnp.int16)),
        (got, tokens, norm_ffn, w_gate_up),
        scratch=[pltpu.VMEM((kv_count * 32, hd), F32)],
    )
    got = exchange(chunk, "kv")
    hidden = exchange(call(activate, shape((kv_count, 16, hd), BF16), (got,)), "kv")
    part = call(
        functools.partial(gathered_dot, w_down.shape[0] // 2 // hd),
        shape((head_count, rows, width), F32),
        (hidden, w_down),
        scratch=[pltpu.VMEM((kv_count * 16, hd), F32)],
    )
    got = exchange(part, "head")
    layer_out = call(close, shape((steps, rollouts, width), BF16), (resid, got))
    return (layer_out, stored)


def solution(mesh):
    return jax.shard_map(
        shards,
        mesh=mesh,
        in_specs=(
            P(None, None, "kv"),
            P("kv"),
            P("kv"),
            P("kv", "head"),
            P("kv", None, "head"),
            P("head", "kv"),
            P("kv", None, "head"),
            P("head", "kv"),
            P(None, "head", "kv", None),
            P(None, "head", "kv", None),
            P(),
            P(),
        ),
        out_specs=(P(None, None, "kv"), P("kv", None, None, "head", None, None)),
        check_vma=False,
    )
```

```python
import functools

import jax
import jax.numpy as jnp
from jax import lax
from jax.experimental import pallas as pl
from jax.experimental.pallas import tpu as pltpu
from jax.sharding import PartitionSpec as P

D = 8192
EPSILON = 1e-05
NEGATIVE = -1e30
F32 = jnp.float32
BF16 = jnp.bfloat16
LANES = 128
TOP = 32767.0
VMEM = pl.BlockSpec(memory_space=pltpu.VMEM)
ANY = pl.BlockSpec(memory_space=pl.ANY)


def ring(sizes, first):
    major, minor = sizes
    return [
        (a + first[0]) % major * minor + (b + first[1]) % minor
        for a in range(major)
        for b in range(minor)
    ]


FIRST, KV = ring((8, 4), (5, 2)), ring((8, 4), (4, 2))
HEAD = ring((4, 2), (2, 0))
PLACE = [KV.index(device) for device in FIRST]


def exchange(x, axis, order):
    return lax.all_to_all(x, axis, 0, 0, tiled=True, axis_index_groups=[order])


def call(body, out_shape, args, specs=None, scratch=(), limit=24):
    return pl.pallas_call(
        body,
        out_shape=out_shape,
        in_specs=[VMEM] * len(args) if specs is None else specs,
        out_specs=jax.tree.map(lambda _: VMEM, out_shape),
        scratch_shapes=list(scratch),
        compiler_params=pltpu.CompilerParams(vmem_limit_bytes=int(limit * 2**20)),
    )(*args)


def project(
    tokens_at, gain_at, w_query_at, w_kv_at, out, tokens, gain, w_query, w_kv, wide, sems
):
    copies = [
        pltpu.make_async_copy(src, dst, sems.at[i])
        for i, (src, dst) in enumerate(
            ((w_kv_at, w_kv), (tokens_at, tokens), (gain_at, gain), (w_query_at, w_query))
        )
    ]
    for copy in copies:
        copy.start()
    for copy in copies[:3]:
        copy.wait()
    rows = tokens.shape[0] * tokens.shape[1]
    width = tokens.shape[2]
    wide[...] = w_kv[...].astype(F32).reshape(2 * width, LANES)
    flat = tokens[...].astype(F32).reshape(rows, tokens.shape[2])
    normed = (flat * gain[...].astype(F32).reshape(1, -1)).astype(BF16)
    kv = [
        jnp.dot(
            normed, wide[pl.ds(i, width, stride=2), :].astype(BF16), preferred_element_type=F32
        )
        for i in range(2)
    ]
    copies[3].wait()
    q = jnp.dot(normed, w_query[...], preferred_element_type=F32)
    stat = jnp.broadcast_to(jnp.sum(flat * flat, -1, keepdims=True), (rows, LANES))
    for half in range(2):
        for slot in range(8):
            if slot < 4:
                at = (half * 4 + slot) * LANES
                part = q[:, at : at + LANES]
            elif slot == 4:
                part = kv[half]
            else:
                part = stat
            out[pl.ds(half * 8 + slot, rows, stride=16), :] = part


def finish(got, relaid, values, out):
    total = jnp.sum(got[...], 0)
    inv = lax.rsqrt(total[7:8] / D + EPSILON)
    out[...] = jnp.broadcast_to((total * inv).astype(BF16)[None], out.shape)


def attend(lengths, owner, whole, keys, values, out, stored):
    rollouts, span, hd = keys.shape
    index = lax.axis_index("kv")
    live = lengths[...].reshape(1, rollouts) - index * span
    holder = owner[...].reshape(1, 2) == index
    scale = hd ** (-0.5)
    row = lax.broadcasted_iota(jnp.int32, (8, LANES), 0)
    lane = lax.broadcasted_iota(jnp.int32, (16, LANES), 1)
    column = lax.broadcasted_iota(jnp.int32, (16, span), 1)
    step = lax.broadcasted_iota(jnp.int32, (16, 1), 0) // 8
    here = index == 0
    queries, news = [], []
    for b in range(rollouts):
        tiles, pairs = [], []
        for s in range(2):
            at = (s * rollouts + b) * 2
            low = whole[PLACE[at]].astype(F32)
            high = whole[PLACE[at + 1]].astype(F32)
            tiles.append(jnp.where(row < 4, low, pltpu.roll(high, 4, 0)))
            pairs.append((low[4:5], high[4:5]))
            pair = jnp.concatenate(pairs[s], 0)
            mine = holder[:, s : s + 1]
            stored[0, s, b, 0] = jnp.where(mine, pair, jnp.zeros_like(pair)).astype(BF16)
        queries.append(jnp.concatenate(tiles, 0))
        news.append(pairs)
    scores = []
    for b in range(rollouts):
        scores.append(
            lax.dot_general(
                queries[b].astype(BF16),
                keys[b],
                (((1,), (1,)), ((), ())),
                preferred_element_type=F32,
            )
            * scale
        )
    weights, totals, tops, extras = [], [], [], []
    for b in range(rollouts):
        keep = column < live[:, b : b + 1]
        masked = jnp.where(keep, scores[b], NEGATIVE)
        top = jnp.max(masked, -1, keepdims=True)
        fresh = []
        for t in range(2):
            allowed = (step >= t) & here
            score = jnp.sum(queries[b] * news[b][t][0], -1, keepdims=True) * scale
            fresh.append((allowed, jnp.where(allowed, score, NEGATIVE)))
            top = jnp.maximum(top, fresh[t][1])
        e = jnp.where(keep, jnp.exp(masked - top), 0.0)
        extra = [jnp.where(ok, jnp.exp(score - top), 0.0) for ok, score in fresh]
        totals.append(jnp.sum(e, -1, keepdims=True) + extra[0] + extra[1])
        weights.append(e.astype(BF16))
        tops.append(top)
        extras.append(extra)
    for b in range(rollouts):
        sums = jnp.dot(weights[b], values[b], preferred_element_type=F32)
        for t in range(2):
            sums = sums + extras[b][t].astype(BF16).astype(F32) * news[b][t][1]
        stat = jnp.where(lane < LANES // 2, tops[b], totals[b])
        for s in range(2):
            sums_s, stat_s = sums[s * 8 : s * 8 + 8], stat[s * 8 : s * 8 + 8]
            at = (s * rollouts + b) * 2
            out[at] = jnp.where(row < 4, sums_s, pltpu.roll(stat_s, 4, 0))
            out[at + 1] = jnp.where(row < 4, pltpu.roll(sums_s, 4, 0), stat_s)


def combine(got, out):
    tops = got[:, 4:, :1]
    factor = jnp.exp(tops - jnp.max(tops, 0, keepdims=True))
    total = jnp.sum(factor * got[:, 4:, LANES // 2 : LANES // 2 + 1], 0)
    context = jnp.sum(factor * got[:, :4, :], 0) / total
    out[...] = jnp.broadcast_to(context.astype(BF16)[None], out.shape)


def gathered_dot(used, whole, w, out, wide):
    chunks, lines = whole.shape[:2]
    wide[...] = whole[...].astype(F32).reshape(chunks * lines, LANES)
    rows = chunks // 2
    parts = [
        wide[pl.ds(half * lines + slot, rows, stride=2 * lines), :].astype(BF16)
        for half in range(2)
        for slot in range(used)
    ]
    part = jnp.dot(jnp.concatenate(parts, 1), w[...], preferred_element_type=F32)
    out[...] = jnp.broadcast_to(part[None], out.shape)


def exponent(x):
    return jnp.ceil(jnp.log2(jnp.maximum(x, 1e-30)))


def gate_up(got, tokens, gain, w, resid_out, out, wide):
    rows, width = resid_out.shape
    resid = tokens[...].astype(F32).reshape(rows, width) + jnp.sum(got[...], 0)
    resid_out[...] = resid
    normed = (resid * gain[...].astype(F32).reshape(1, -1)).astype(BF16)
    stat = jnp.sum(resid * resid, -1, keepdims=True)
    power = exponent(stat)
    scaled = stat * jnp.exp2(-power) * TOP
    high = jnp.floor(scaled)
    low = jnp.floor((scaled - high) * TOP)
    lines = w.shape[2] // 2 // LANES
    across = lines * LANES
    parts = [jnp.dot(normed, w[which], preferred_element_type=F32) for which in range(2)]
    for half in range(2):
        pair = [part[:, half * across : (half + 1) * across] for part in parts]
        size = jnp.maximum(*(jnp.max(jnp.abs(part), -1, keepdims=True) for part in pair))
        shift = exponent(size)
        factor = jnp.exp2(-shift) * TOP
        extras = ((shift, high), (low, power))
        for which in range(2):
            for slot in range(16):
                if slot < lines:
                    line = jnp.floor(
                        pair[which][:, slot * LANES : (slot + 1) * LANES] * factor + 0.5
                    )
                    line = jnp.clip(line, -TOP, TOP)
                else:
                    line = jnp.broadcast_to(extras[which][slot - lines], (rows, LANES))
                wide[pl.ds(half * 32 + which * 16 + slot, rows, stride=64), :] = line
    out[...] = wide[...].astype(jnp.int32).astype(jnp.int16).reshape(out.shape)


def activate(got, out):
    coded = got[...].astype(jnp.int32).astype(F32)
    total = jnp.sum(coded * (jnp.exp2(coded[:, 14:15]) / TOP), 0)
    stats = (coded[:, 15:16] + coded[:, 30:31] / TOP) * (jnp.exp2(coded[:, 31:32]) / TOP)
    inv = lax.rsqrt(jnp.sum(stats, 0) / D + EPSILON)
    gate, up = total[:16] * inv, total[16:] * inv
    hidden = (gate * jax.nn.sigmoid(gate) * up).astype(BF16)
    out[...] = jnp.broadcast_to(hidden[None], out.shape)


def close(resid, got, out):
    total = resid[...] + jnp.sum(got[...], 0)
    out[...] = total.astype(BF16).reshape(out.shape)


def shards(
    tokens,
    norm_attn,
    norm_ffn,
    w_query,
    w_kv,
    w_out,
    w_gate_up,
    w_down,
    cache_keys,
    cache_values,
    lengths,
    owner,
):
    kv_count = lax.axis_size("kv")
    head_count = lax.axis_size("head")
    steps, rollouts, width = tokens.shape
    rows = steps * rollouts
    span, hd = cache_keys.shape[2:]
    shape = jax.ShapeDtypeStruct
    w_gate_up = w_gate_up.transpose(1, 0, 2)

    chunk = call(
        project,
        shape((kv_count * 8, hd), F32),
        (tokens, norm_attn, w_query, w_kv),
        [ANY] * 4,
        [pltpu.VMEM(x.shape, x.dtype) for x in (tokens, norm_attn, w_query, w_kv)]
        + [pltpu.VMEM((2 * width, hd), F32), pltpu.SemaphoreType.DMA((4,))],
        60,
    )
    got = exchange(chunk.reshape(kv_count, 8, hd), "kv", FIRST)
    cache_shape = (rollouts, span, hd)
    keys, values = cache_keys.reshape(cache_shape), cache_values.reshape(cache_shape)
    mine = call(
        finish,
        shape((kv_count, 8, hd), BF16),
        (got, w_gate_up, values),
        [VMEM, ANY, VMEM],
        limit=51,
    )
    whole = exchange(mine, "kv", KV)

    chunk, stored = call(
        attend,
        (shape((kv_count, 8, hd), F32), shape((1, steps, rollouts, 1, 2, hd), BF16)),
        (lengths, owner, whole, keys, values),
        [VMEM] * 5,
    )
    got = exchange(chunk, "kv", KV)
    context = exchange(call(combine, shape((kv_count, 4, hd), BF16), (got,)), "kv", KV)
    part = call(
        functools.partial(gathered_dot, 4),
        shape((head_count, rows, width), F32),
        (context, w_out),
        scratch=[pltpu.VMEM((kv_count * 4, hd), F32)],
    )
    got = exchange(part, "head", HEAD)

    resid, chunk = call(
        gate_up,
        (shape((rows, width), F32), shape((kv_count, 32, hd), jnp.int16)),
        (got, tokens, norm_ffn, w_gate_up),
        scratch=[pltpu.VMEM((kv_count * 32, hd), F32)],
    )
    got = exchange(chunk, "kv", KV)
    hidden = exchange(call(activate, shape((kv_count, 16, hd), BF16), (got,)), "kv", KV)
    part = call(
        functools.partial(gathered_dot, w_down.shape[0] // 2 // hd),
        shape((head_count, rows, width), F32),
        (hidden, w_down),
        scratch=[pltpu.VMEM((kv_count * 16, hd), F32)],
    )
    got = exchange(part, "head", HEAD)
    layer_out = call(close, shape((steps, rollouts, width), BF16), (resid, got))
    return (layer_out, stored)


def solution(mesh):
    return jax.shard_map(
        shards,
        mesh=mesh,
        in_specs=(
            P(None, None, "kv"),
            P("kv"),
            P("kv"),
            P("kv", "head"),
            P("kv", None, "head"),
            P("head", "kv"),
            P("kv", None, "head"),
            P("head", "kv"),
            P(None, "head", "kv", None),
            P(None, "head", "kv", None),
            P(),
            P(),
        ),
        out_specs=(P(None, None, "kv"), P("kv", None, None, "head", None, None)),
        check_vma=False,
    )
```
